256 devices in a mesh: dp: 16 (over z, core), rows: 4 (over x), heads: 4 (over y).
Axes of the slice: x: 4, y: 4, z: 8, core: 2. Of those that a mesh axis runs over, the one named last changes fastest.
Arguments:
- hidden: bfloat16 [16, 16, 2048], P('dp'), may hold values from -458.54834 to 458.54834
- norm_gain: float32 [1, 2048], replicated, may hold values from 0.25 to 1.75
- query_weight: bfloat16 [1, 2048, 4096], P(None, None, ('heads', 'rows')), may hold values from -0.125 to 0.125
- key_weight: bfloat16 [1, 2048, 4096], P(None, None, ('heads', 'rows')), may hold values from -0.125 to 0.125
- value_weight: bfloat16 [1, 2048, 4096], P(None, None, ('heads', 'rows')), may hold values from -0.125 to 0.125
- zgate_weight: bfloat16 [1, 2048, 4096], P(None, None, ('heads', 'rows')), may hold values from -0.125 to 0.125
- gate_weight: bfloat16 [1, 2, 2048, 4], P(None, None, None, 'heads'), may hold values from -0.125 to 0.125
- decay_rate: float32 [1, 4], P(None, 'heads'), may hold values from 0.005 to 0.5
- output_gain: float32 [1, 1024], P(None, 'rows'), may hold values from 0.25 to 1.75
- output_weight: bfloat16 [1, 4096, 2048], P(None, ('heads', 'rows')), may hold values from -0.09375 to 0.09375
- recurrent_state: float32 [1, 16, 4, 1024, 1024], P(None, 'dp', 'heads', 'rows'), may hold values from -6 to 6
- final_gain: float32 [2048], replicated, may hold values from 0.25 to 1.75
- vocab_weight: bfloat16 [2048, 131072], P(None, ('dp', 'rows', 'heads')), may hold values from -7.9549513 to 7.9549513
Outputs:
- next_state: float32 [1, 16, 4, 1024, 1024], P(None, 'dp', 'heads', 'rows')
- log_probs: float32 [16, 16, 131072], P(None, None, ('dp', 'rows', 'heads'))
The draws below stay inside these ranges and needn't reach their ends.
All inputs are finite; a program needn't handle non-finite values.
Results may differ from the reference program's by a relative error of at most 0.0024.
The reference program's roundings to bfloat16 on the way (of `normed_in`, `gated` and `final_in`) count: a program that leaves them out, or rounds other values in their place, can miss the bound.
Values may be sent and summed in bfloat16 or wider, within the bound.
No kernel may reach another device: no remote copies, remote signals or barrier semaphores. Data moves between devices by JAX's collectives and lax.ppermute only.
A program may use at most 64 MiB of HBM per device.

```python
import math
import jax
import jax.numpy as jnp
from jax import lax

D = 2048
H = 4
DK = 1024
DV = 1024
LAYERS = 1
TOKS = 16
V = 131072
SEQS = 16


def loud_feature(key):
    return jax.random.randint(jax.random.fold_in(key, 911), (), 0, D)


def draw_hidden(key, part):
    loud = loud_feature(key)
    keys = jax.random.split(jax.random.fold_in(key, 17), 4)
    base = jnp.clip(jax.random.normal(keys[0], (SEQS, TOKS, D), jnp.float32), -6.0, 6.0)
    picked = jax.random.randint(keys[1], (SEQS, TOKS), 0, 4) == 0
    picked = jnp.logical_or(picked, (jnp.arange(TOKS) == 0)[None, :])
    amount = jnp.exp(jax.random.uniform(keys[2], (SEQS, TOKS), jnp.float32, math.log(3.0), math.log(10.0))) * math.sqrt(D)
    signs = jnp.where(jax.random.randint(keys[3], (SEQS, TOKS), 0, 2) == 0, -1.0, 1.0)
    spike = jnp.where(picked, amount * signs, 0.0)
    onehot = (jnp.arange(D) == loud).astype(jnp.float32)
    return (base + spike[..., None] * onehot).astype(jnp.bfloat16)


def draw_vocab_weight(key, part):
    loud = loud_feature(key)
    keys = jax.random.split(jax.random.fold_in(key, 23), 2)
    base = jnp.clip(jax.random.normal(keys[0], (D, V), jnp.float32), -6.0, 6.0)
    loud_row = jnp.clip(jax.random.normal(keys[1], (1, V), jnp.float32), -6.0, 6.0)
    drawn = base * (D / 9.0) ** (-0.5)
    strong = loud_row * (60.0 / math.sqrt(D))
    chosen = (jnp.arange(D) == loud)[:, None]
    return jnp.where(chosen, strong, drawn).astype(jnp.bfloat16)


def level_of(key, dims, cuts, least, largest):
    level = 1.0
    for dim, parts in cuts:
        steps = jax.random.uniform(jax.random.fold_in(jax.random.fold_in(key, 6), dim), (parts,), jnp.float32, least / len(cuts), largest / len(cuts))
        level = level * jnp.repeat(jnp.exp(steps), dims[dim] // parts).reshape((-1,) + (1,) * (len(dims) - 1 - dim))
    return level


def centred(stream_key, dims, deviation, reach, cuts=(), held_as=jnp.bfloat16):
    entries = jax.random.normal(stream_key, dims, jnp.float32) * deviation
    if len(cuts) > 0:
        entries = level_of(stream_key, dims, cuts, -0.22, 0.18) * entries
    return jnp.clip(entries, min=-reach, max=reach).astype(held_as)


def setup_inputs(seed: int = 0) -> dict:
    splits = jax.random.split(jax.random.key(seed), 14)
    return {
        "hidden": draw_hidden(jax.random.fold_in(splits[13], 71), 0),
        "norm_gain": jnp.clip(1.0 + 0.15 * jax.random.normal(splits[1], (LAYERS, D), jnp.float32), 0.25, 1.75),
        "query_weight": centred(splits[2], (LAYERS, D, H * DK), D ** -0.5, 0.125, ((2, 16),)),
        "key_weight": centred(splits[3], (LAYERS, D, H * DK), D ** -0.5, 0.125, ((2, 16),)),
        "value_weight": centred(splits[4], (LAYERS, D, H * DV), D ** -0.5, 0.125, ((2, 16),)),
        "zgate_weight": centred(splits[5], (LAYERS, D, H * DV), D ** -0.5, 0.125, ((2, 16),)),
        "gate_weight": centred(splits[6], (LAYERS, 2, D, H), D ** -0.5, 0.125, ((3, 4),)),
        "decay_rate": jnp.clip(jnp.exp(math.log(0.5) - 4.6051702 * jax.random.uniform(splits[7], (LAYERS, H), jnp.float32) ** level_of(splits[7], (LAYERS, H), ((1, 4),), -0.2, 0.2)), 0.005, 0.5),
        "output_gain": jnp.clip(1.0 + 0.15 * jax.random.normal(splits[8], (LAYERS, DV), jnp.float32), 0.25, 1.75),
        "output_weight": centred(splits[9], (LAYERS, H * DV, D), (H * DV) ** -0.5, 0.09375, ((1, 16),)),
        "recurrent_state": centred(splits[10], (LAYERS, SEQS, H, DK, DV), 1.0, 6.0, ((1, 16), (2, 4), (3, 4)), jnp.float32),
        "final_gain": jnp.clip(1.0 + 0.15 * jax.random.normal(splits[11], (D,), jnp.float32), 0.25, 1.75),
        "vocab_weight": draw_vocab_weight(jax.random.fold_in(splits[13], 71), 0),
    }


epsilon = 1e-06

def rms_norm(values, gain):
    return values * lax.rsqrt(lax.optimization_barrier(jnp.mean(values * values, axis=-1, keepdims=True)) + epsilon) * gain

def reference(hidden, norm_gain, query_weight, key_weight, value_weight, zgate_weight, gate_weight, decay_rate, output_gain, output_weight, recurrent_state, final_gain, vocab_weight):
    highest_score = lax.Precision.HIGHEST
    stream = hidden.astype(jnp.float32)
    states_out = []
    for layer_idx in range(LAYERS):
        normed_in = rms_norm(stream, norm_gain[layer_idx]).astype(jnp.bfloat16)
        flat = normed_in.reshape(-1, D)

        def project(weight, size):
            return jnp.dot(flat, weight[layer_idx], preferred_element_type=jnp.float32).reshape(SEQS, TOKS, H, size)
        query = project(query_weight, DK)
        key = project(key_weight, DK)
        value = project(value_weight, DV)
        zgate = project(zgate_weight, DV)
        gates = jnp.einsum('md,gdh->gmh', flat.astype(jnp.float32), gate_weight[layer_idx].astype(jnp.float32), precision=highest_score)
        gates = gates.reshape(2, SEQS, TOKS, H)
        log_decay = -decay_rate[layer_idx] * jax.nn.softplus(gates[0])
        strength = jax.nn.sigmoid(gates[1])
        query = query * lax.rsqrt(lax.optimization_barrier(jnp.sum(query * query, axis=-1, keepdims=True)) + epsilon) * DK ** (-0.5)
        key = key * lax.rsqrt(lax.optimization_barrier(jnp.sum(key * key, axis=-1, keepdims=True)) + epsilon)

        def advance(carry, inputs):
            query_t, key_t, value_t, decay_t, strength_t = inputs
            carry = jnp.exp(decay_t)[..., None, None] * carry
            guess = jnp.einsum('shk,shkv->shv', key_t, carry, precision=highest_score)
            update = strength_t[..., None] * (value_t - guess)
            carry = carry + key_t[..., :, None] * update[..., None, :]
            readout = jnp.einsum('shk,shkv->shv', query_t, carry, precision=highest_score)
            return (carry, readout)
        inputs = tuple((jnp.moveaxis(item, 1, 0) for item in (query, key, value, log_decay, strength)))
        final_state, readouts = lax.scan(advance, recurrent_state[layer_idx], inputs)
        readouts = jnp.moveaxis(readouts, 0, 1)
        gated = (rms_norm(readouts, output_gain[layer_idx]) * jax.nn.silu(zgate)).astype(jnp.bfloat16)
        mixed = jnp.dot(gated.reshape(-1, H * DV), output_weight[layer_idx], preferred_element_type=jnp.float32)
        stream = stream + mixed.reshape(SEQS, TOKS, D)
        states_out.append(final_state)
    final_in = rms_norm(stream, final_gain).astype(jnp.bfloat16)
    logits = jnp.dot(final_in.reshape(-1, D), vocab_weight, preferred_element_type=jnp.float32)
    row_peak = lax.optimization_barrier(jnp.max(logits, axis=-1, keepdims=True))
    log_total = row_peak + jnp.log(lax.optimization_barrier(jnp.sum(jnp.exp(logits - row_peak), axis=-1, keepdims=True)))
    log_probs = (logits - log_total).reshape(SEQS, TOKS, V)
    return (jnp.stack(states_out), log_probs)
```

```python
import jax
import jax.numpy as jnp
from jax import lax
from jax.sharding import Mesh
from jax.sharding import PartitionSpec as P

DK = 1024
Z, C, X, Y = ("dp_0", "dp_1", "rows", "heads")
DP = (Z, C)
ALL = (Z, C, X, Y)

epsilon = 1e-06


def exchanged(parts, axes):
    return lax.all_to_all(parts, axes, 0, 0, tiled=True)


def sent_to_all(shard, axes):
    size = lax.axis_size(axes)
    return exchanged(jnp.broadcast_to(shard[None], (size, *shard.shape)), axes)


def shifted(shard, axis, step):
    size = lax.axis_size(axis)
    return lax.ppermute(shard, axis, [(i, (i + step) % size) for i in range(size)])


def rms_norm(values, gain):
    return values * lax.rsqrt(jnp.mean(values * values, axis=-1, keepdims=True) + epsilon) * gain


def on_device(
    hidden,
    norm_gain,
    query_weight,
    key_weight,
    value_weight,
    zgate_weight,
    gate_weight,
    decay_rate,
    output_gain,
    output_weight,
    recurrent_state,
    final_gain,
    vocab_weight,
):
    highest = lax.Precision.HIGHEST
    f32, bf16 = jnp.float32, jnp.bfloat16
    _, tokens, width = hidden.shape
    stream = hidden[0].astype(f32)
    positions = jnp.arange(tokens)
    causal = positions[:, None] >= positions[None, :]
    strictly = positions[:, None] > positions[None, :]
    normed_in = rms_norm(stream, norm_gain[0]).astype(bf16)

    def project(weight):
        return jnp.dot(normed_in, weight[0], preferred_element_type=f32)

    query, key, value = project(query_weight), project(key_weight), project(value_weight)
    columns = value.shape[1]
    state = recurrent_state[0, 0, 0]
    both = jnp.concatenate([key, query], axis=0)
    lookups = jnp.dot(both, state, precision=highest)
    grams = jnp.dot(both, key.T, precision=highest)
    query_length = jnp.sum(query * query, axis=-1)
    own = jnp.concatenate(
        [
            lookups,
            jnp.concatenate(
                [
                    value,
                    jnp.concatenate(
                        [
                            grams[:tokens],
                            grams[tokens:],
                            query_length[:, None],
                            jnp.zeros((tokens, columns - 2 * tokens - 1), f32),
                        ],
                        axis=1,
                    ),
                ],
                axis=0,
            ),
        ],
        axis=1,
    )
    others = [shifted(own, X, k) for k in (1, 3, 2)]
    zgate = project(zgate_weight)
    gates = jnp.dot(normed_in, gate_weight[0, :, :, 0].T, preferred_element_type=f32)
    log_decay = -decay_rate[0, 0] * jax.nn.softplus(gates[:, 0])
    strength = jax.nn.sigmoid(gates[:, 1])
    row = lax.axis_index(X)
    total = own + others[0] + others[1] + others[2]
    values_full = jnp.zeros((tokens, DK), f32)
    for piece, step in zip([own] + others, (0, 1, 3, 2)):
        source = (row - step) % 4
        values_full = lax.dynamic_update_slice(
            values_full, piece[:tokens, DK : DK + columns], (0, source * columns)
        )
    key_lookups, query_lookups = total[:tokens, :DK], total[tokens:, :DK]
    key_gram = total[tokens:, DK : DK + tokens]
    cross_gram = total[tokens:, DK + tokens : DK + 2 * tokens]
    query_length = total[tokens:, DK + 2 * tokens]
    key_length = jnp.diagonal(key_gram)
    query_scale = lax.rsqrt(query_length + epsilon) * DK ** (-0.5)
    key_scale = lax.rsqrt(key_length + epsilon)
    normalized_key = key * key_scale[:, None]
    key_lookups = key_lookups * key_scale[:, None]
    query_lookups = query_lookups * query_scale[:, None]
    key_gram = key_gram * key_scale[:, None] * key_scale[None, :]
    cross_gram = cross_gram * query_scale[:, None] * key_scale[None, :]
    log_gates = jnp.cumsum(log_decay)
    spacing = log_gates[:, None] - log_gates[None, :]
    ratio = jnp.where(causal, jnp.exp(jnp.where(causal, spacing, 0.0)), 0.0)
    lower = jnp.where(strictly, strength[:, None] * ratio * key_gram, 0.0)
    right_side = strength[:, None] * (values_full - jnp.exp(log_gates)[:, None] * key_lookups)
    system = jnp.eye(tokens, dtype=f32) + lower
    updates = lax.linalg.triangular_solve(
        system, right_side, left_side=True, lower=True, unit_diagonal=True
    )
    readouts = jnp.exp(log_gates)[:, None] * query_lookups + jnp.dot(
        ratio * cross_gram, updates, precision=highest
    )
    leftover = jnp.exp(log_gates[-1] - log_gates)
    new_state = jnp.exp(log_gates[-1]) * state + jnp.dot(
        normalized_key.T, leftover[:, None] * updates, precision=highest
    )
    readout_piece = lax.dynamic_slice_in_dim(readouts, row * columns, columns, 1)
    inverse = lax.rsqrt(jnp.mean(readouts * readouts, axis=-1, keepdims=True) + epsilon)
    gated = (readout_piece * inverse * output_gain[0] * jax.nn.silu(zgate)).astype(bf16)
    partial = jnp.dot(gated, output_weight[0], preferred_element_type=f32)
    summed = jnp.sum(exchanged(partial.reshape(tokens, 16, width // 16), (X, Y)), axis=0)
    token = row * lax.axis_size(Y) + lax.axis_index(Y)
    mine = lax.dynamic_index_in_dim(stream, token, 0, keepdims=False).reshape(16, -1) + summed
    final_in = mine * lax.rsqrt(jnp.mean(mine * mine) + epsilon) * final_gain.reshape(16, -1)
    final_in = final_in.astype(bf16)
    column = sent_to_all(final_in, Z).reshape(-1, width)
    near = sent_to_all(column, (X, Y)).reshape(-1, width)
    far = shifted(near, C, 1)

    def scores(inputs):
        logits = jnp.dot(inputs, vocab_weight, preferred_element_type=f32)
        peak = jnp.max(logits, axis=-1)
        return logits, peak + jnp.log(jnp.sum(jnp.exp(logits - peak[:, None]), axis=-1))

    near_logits, near_lse = scores(near)
    far_logits, far_lse = scores(far)
    core = lax.axis_index(C)
    lse = jnp.stack([near_lse, far_lse])
    other = shifted(lse, C, 1)[::-1]
    peak = jnp.maximum(lse, other)
    chip = peak + jnp.log(jnp.exp(lse - peak) + jnp.exp(other - peak))
    chip = jnp.where(core == 0, chip, chip[::-1])
    everyone = sent_to_all(chip, (Z, X, Y))
    peak = jnp.max(everyone, axis=0)
    total = peak + jnp.log(jnp.sum(jnp.exp(everyone - peak), axis=0))
    even = jnp.where(core == 0, near_logits, far_logits)
    odd = jnp.where(core == 0, far_logits, near_logits)
    log_probs = jnp.stack([even, odd]) - total[:, :, None]
    zs = lax.axis_size(Z)
    log_probs = log_probs.reshape(2, tokens, zs, -1).transpose(2, 0, 1, 3)
    return (new_state[None, None, None], log_probs.reshape(2 * zs, tokens, -1))


def solution(mesh):
    split = Mesh(
        mesh.devices.reshape(8, 2, mesh.shape["rows"], mesh.shape["heads"]),
        ALL,
    )
    return jax.shard_map(
        on_device,
        mesh=split,
        in_specs=(
            P(DP, None, None),
            P(),
            P(None, None, (Y, X)),
            P(None, None, (Y, X)),
            P(None, None, (Y, X)),
            P(None, None, (Y, X)),
            P(None, None, None, Y),
            P(None, Y),
            P(None, X),
            P(None, (Y, X), None),
            P(None, DP, Y, X, None),
            P(),
            P(None, ALL),
        ),
        out_specs=(P(None, DP, Y, X, None), P(None, None, ALL)),
        check_vma=False,
    )
```

```python
import jax
import jax.numpy as jnp
from jax import lax
from jax.experimental import pallas as pl
from jax.experimental.pallas import tpu as pltpu
from jax.sharding import Mesh
from jax.sharding import PartitionSpec as P

Z, C, X, Y = ("dp_0", "dp_1", "rows", "heads")
DP = (Z, C)
ALL = (Z, C, X, Y)

TOKS = 16
DK = 1024
LANES = 128
epsilon = 1e-06
f32, bf16 = jnp.float32, jnp.bfloat16
HIGHEST = lax.Precision.HIGHEST

VM = pl.BlockSpec(memory_space=pltpu.VMEM)
SM = pl.BlockSpec(memory_space=pltpu.SMEM)
HB = pl.BlockSpec(memory_space=pl.ANY)


def exchanged(parts, axes):
    return lax.all_to_all(parts, axes, 0, 0, tiled=True)


def shifted(shard, axis, step):
    size = lax.axis_size(axis)
    return lax.ppermute(shard, axis, [(i, (i + step) % size) for i in range(size)])


def shape(dims, dtype=f32):
    return jax.ShapeDtypeStruct(dims, dtype)


def params(mib):
    return pltpu.CompilerParams(vmem_limit_bytes=mib << 20)


def cost(flops, size):
    return pl.CostEstimate(flops=flops, bytes_accessed=size, transcendentals=0)


def across(a, b):
    return lax.dot_general(
        a, b, (((1,), (1,)), ((), ())), precision=HIGHEST, preferred_element_type=f32
    )


def halves(a):
    high = a.astype(bf16)
    return high, (a - high.astype(f32)).astype(bf16)


def project_kernel(
    hidden, gain, key_w, query_w, value_w, state, own, normed, key_out,
    key_v, query_v, value_v, state_v, sems,
):
    copies = [
        pltpu.make_async_copy(src, dst, sems.at[i])
        for i, (src, dst) in enumerate(
            ((key_w, key_v), (query_w, query_v), (state, state_v), (value_w, value_v))
        )
    ]
    for copy in copies:
        copy.start()
    x = hidden[...].astype(f32)
    inverse = lax.rsqrt(jnp.mean(x * x, axis=-1, keepdims=True) + epsilon)
    inputs = (x * inverse * gain[...]).astype(bf16)
    normed[...] = inputs
    copies[0].wait()
    key = jnp.dot(inputs, key_v[...], preferred_element_type=f32)
    key_out[...] = key
    copies[1].wait()
    query = jnp.dot(inputs, query_v[...], preferred_element_type=f32)
    both = jnp.concatenate([key, query], axis=0)
    wide_key = jnp.concatenate([key, jnp.zeros((LANES - TOKS, key.shape[1]), f32)], axis=0)
    grams = across(both, wide_key)
    length = jnp.sum(query * query, axis=-1, keepdims=True)
    lane = lax.broadcasted_iota(jnp.int32, (TOKS, LANES), 1)
    own[TOKS:, DK : DK + LANES] = jnp.where(lane == TOKS, length, grams[:TOKS])
    own[TOKS:, DK + LANES :] = grams[TOKS:]
    high, low = halves(both)
    copies[2].wait()
    state_high, state_low = halves(state_v[...])
    first = jnp.dot(jnp.concatenate([high, low], axis=0), state_high, preferred_element_type=f32)
    second = jnp.dot(high, state_low, preferred_element_type=f32)
    own[:, :DK] = first[: 2 * TOKS] + first[2 * TOKS :] + second
    copies[3].wait()
    own[:TOKS, DK:] = jnp.dot(inputs, value_v[...], preferred_element_type=f32)


def gate_kernel(normed, zgate_w, gate_w, rate, hidden, silu, aux, mine, wide):
    inputs = normed[...]
    z = jnp.dot(inputs, zgate_w[...], preferred_element_type=f32)
    silu[...] = z * jax.nn.sigmoid(z)
    inputs = inputs.astype(f32)
    gates = gate_w[...].astype(f32)
    decay_in = jnp.sum(inputs * gates[0:1], axis=-1, keepdims=True)
    strength = jax.nn.sigmoid(jnp.sum(inputs * gates[1:2], axis=-1, keepdims=True))
    softplus = jnp.maximum(decay_in, 0.0) + jnp.log1p(jnp.exp(-jnp.abs(decay_in)))
    decay = -rate[0, 0] * softplus
    t = lax.broadcasted_iota(jnp.int32, (TOKS, LANES), 0)
    j = lax.broadcasted_iota(jnp.int32, (TOKS, LANES), 1)
    decay_row = jnp.sum(jnp.where(t == j, decay, 0.0), axis=0, keepdims=True)
    log_col = jnp.sum(jnp.where(j <= t, decay_row, 0.0), axis=1, keepdims=True)
    log_row = jnp.sum(jnp.where(t <= j, decay, 0.0), axis=0, keepdims=True)
    causal = j <= t
    ratio = jnp.where(causal, jnp.exp(jnp.where(causal, log_col - log_row, 0.0)), 0.0)
    last = jnp.sum(decay, axis=0, keepdims=True)
    ones = jnp.ones((TOKS, LANES), f32)
    aux[0] = jnp.where(j < t, strength * ratio, 0.0)
    aux[1] = ratio
    aux[2] = strength * ones
    aux[3] = jnp.exp(log_col) * ones
    aux[4] = jnp.exp(last - log_col) * ones
    aux[5] = jnp.exp(last) * ones
    token = lax.axis_index(X) * lax.axis_size(Y) + lax.axis_index(Y)
    wide[...] = hidden[...].astype(f32)
    row = wide[pl.ds(token, 1), :]
    for k in range(16):
        mine[k : k + 1, :] = row[:, k * LANES : (k + 1) * LANES]


def solve_kernel(
    own, one, three, two, silu, aux, gain, out_w, message, updates, key_scale_out,
    values, reads,
):
    columns = silu.shape[1]
    place = lax.axis_index(X)
    for piece, step in ((own, 0), (one, 1), (three, 3), (two, 2)):
        source = lax.rem(place - step + 4, 4)
        values[:, pl.ds(pl.multiple_of(source * columns, columns), columns)] = piece[:TOKS, DK:]
    total = (own[:, :DK] + two[:, :DK]) + (one[:, :DK] + three[:, :DK])
    grams = (own[TOKS:, DK:] + two[TOKS:, DK:]) + (one[TOKS:, DK:] + three[TOKS:, DK:])
    key_gram, cross_gram = grams[:, :LANES], grams[:, LANES:]
    t = lax.broadcasted_iota(jnp.int32, (TOKS, LANES), 0)
    j = lax.broadcasted_iota(jnp.int32, (TOKS, LANES), 1)
    diagonal = jnp.where(t == j, key_gram, 0.0)
    key_col = lax.rsqrt(jnp.sum(diagonal, axis=1, keepdims=True) + epsilon)
    key_row = lax.rsqrt(jnp.sum(diagonal, axis=0, keepdims=True) + epsilon)
    length = jnp.sum(jnp.where(j == TOKS, key_gram, 0.0), axis=1, keepdims=True)
    query_col = lax.rsqrt(length + epsilon) * DK ** (-0.5)
    key_scale_out[...] = key_col * jnp.ones((TOKS, LANES), f32)
    lower = aux[0] * key_gram * key_col * key_row
    mixing = aux[1] * cross_gram * query_col * key_row
    strength, grown, leftover = aux[2][:, :1], aux[3][:, :1], aux[4][:, :1]
    rest = strength * (values[...] - grown * (total[:TOKS] * key_col))
    readout = grown * (total[TOKS:] * query_col)
    solved = []
    for k in range(TOKS):
        update = rest[k : k + 1]
        solved.append(update)
        if k < TOKS - 1:
            rest = rest - lower[:, k : k + 1] * update
        readout = readout + mixing[:, k : k + 1] * update
    updates[...] = leftover * jnp.concatenate(solved, axis=0)
    reads[...] = readout
    inverse = lax.rsqrt(jnp.mean(readout * readout, axis=-1, keepdims=True) + epsilon)
    piece = reads[:, pl.ds(pl.multiple_of(place * columns, columns), columns)]
    gated = (piece * inverse * gain[...] * silu[...]).astype(bf16)
    partial = jnp.dot(gated, out_w[...], preferred_element_type=f32)
    for k in range(16):
        message[:, k, :] = partial[:, k * LANES : (k + 1) * LANES]


def final_kernel(parts, mine, gain, out):
    stream = mine[...] + jnp.sum(parts[...], axis=0)
    inverse = lax.rsqrt(jnp.sum(stream * stream, keepdims=True) / (16 * LANES) + epsilon)
    final = (stream * inverse * gain[...]).astype(bf16)
    for k in range(out.shape[0]):
        out[k] = final


def spread_kernel(column, out, wide):
    wide[...] = column[...].astype(f32)
    rows = jnp.concatenate([wide[:, k, :] for k in range(16)], axis=1).astype(bf16)
    for k in range(out.shape[0]):
        out[k] = rows


def near_kernel(inputs, vocab_w, logits, lse):
    result = jnp.dot(inputs[...], vocab_w[...], preferred_element_type=f32)
    logits[...] = result
    peak = jnp.max(result, axis=-1, keepdims=True)
    total = peak + jnp.log(jnp.sum(jnp.exp(result - peak), axis=-1, keepdims=True))
    lse[...] = jnp.transpose(jnp.broadcast_to(total, (LANES, LANES)))[:8]


def far_kernel(inputs, vocab_w, near_lse, logits, lse):
    result = jnp.dot(inputs[...], vocab_w[...], preferred_element_type=f32)
    logits[...] = result
    peak = jnp.max(result, axis=-1, keepdims=True)
    total = peak + jnp.log(jnp.sum(jnp.exp(result - peak), axis=-1, keepdims=True))
    lse[0:1] = near_lse[0:1]
    lse[1:2] = jnp.transpose(jnp.broadcast_to(total, (LANES, LANES)))[0:1]


def chip_kernel(mine, other, out):
    core = lax.axis_index(C)
    a = mine[...]
    b = jnp.concatenate([other[1:2], other[0:1]], axis=0)
    peak = jnp.maximum(a, b)
    both = peak + jnp.log(jnp.exp(a - peak) + jnp.exp(b - peak))
    both = jnp.where(core == 0, both, jnp.concatenate([both[1:2], both[0:1]], axis=0))
    out[...] = jnp.broadcast_to(both[None], out.shape)


def score_kernel(everyone, near, far, out, wide):
    core = lax.axis_index(C)
    parts = everyone[...]
    peak = jnp.max(parts, axis=0)
    total = peak + jnp.log(jnp.sum(jnp.exp(parts - peak[None]), axis=0))
    total = jnp.where(core == 0, total, jnp.concatenate([total[1:2], total[0:1]], axis=0))
    for k, logits in enumerate((near, far)):
        column = jnp.transpose(jnp.broadcast_to(total[k : k + 1], (LANES, LANES)))
        for m in range(logits.shape[1] // LANES):
            cut = slice(m * LANES, (m + 1) * LANES)
            wide[4 * k + m] = logits[:, cut] - column
        half = core if k == 0 else 1 - core
        for z in range(8):
            for m in range(logits.shape[1] // LANES):
                cut = slice(m * LANES, (m + 1) * LANES)
                out[2 * z + half, :, cut] = wide[4 * k + m, pl.ds(z, TOKS, stride=8), :]


def on_device(
    hidden,
    norm_gain,
    query_weight,
    key_weight,
    value_weight,
    zgate_weight,
    gate_weight,
    decay_rate,
    output_gain,
    output_weight,
    recurrent_state,
    final_gain,
    vocab_weight,
):
    hidden = hidden[0]
    width = hidden.shape[1]
    columns = query_weight.shape[2]
    state = recurrent_state[0, 0, 0]
    vocab = vocab_weight.shape[1]
    own, normed, key = pl.pallas_call(
        project_kernel,
        out_shape=(
            shape((2 * TOKS, DK + columns)),
            shape((TOKS, width), bf16),
            shape((TOKS, columns)),
        ),
        in_specs=[VM, VM, HB, HB, HB, HB],
        out_specs=(VM, VM, VM),
        scratch_shapes=[
            pltpu.VMEM((width, columns), bf16),
            pltpu.VMEM((width, columns), bf16),
            pltpu.VMEM((width, columns), bf16),
            pltpu.VMEM(state.shape, f32),
            pltpu.SemaphoreType.DMA((4,)),
        ],
        compiler_params=params(16),
        name="project",
    )(hidden, norm_gain, key_weight[0], query_weight[0], value_weight[0], state)
    one, three, two = [shifted(own, X, k) for k in (1, 3, 2)]
    silu, aux, mine = pl.pallas_call(
        gate_kernel,
        out_shape=(shape((TOKS, columns)), shape((6, TOKS, LANES)), shape((16, LANES))),
        in_specs=[VM, VM, VM, SM, VM],
        out_specs=(VM, VM, VM),
        scratch_shapes=[pltpu.VMEM((TOKS, width), f32)],
        compiler_params=params(8),
        cost_estimate=cost(16 * 2048 * 512, 1 << 21),
        name="gates",
    )(normed, zgate_weight[0], gate_weight[0, :, :, 0], decay_rate, hidden)
    message, updates, key_scale = pl.pallas_call(
        solve_kernel,
        out_shape=(
            shape((TOKS, 16, LANES)),
            shape((TOKS, DK)),
            shape((TOKS, LANES)),
        ),
        in_specs=[VM] * 8,
        out_specs=(VM, VM, VM),
        scratch_shapes=[pltpu.VMEM((TOKS, DK), f32), pltpu.VMEM((TOKS, DK), f32)],
        compiler_params=params(8),
        name="solve",
    )(own, one, three, two, silu, aux, output_gain, output_weight[0])
    parts = exchanged(message, (X, Y))
    new_state = aux[5, 0, 0] * state + jnp.dot(
        (key * key_scale[:, :1]).T, updates, precision=HIGHEST
    )
    final_in = pl.pallas_call(
        final_kernel,
        out_shape=shape((8, 16, LANES), bf16),
        in_specs=[VM] * 3,
        out_specs=VM,
        name="final_norm",
    )(parts, mine, final_gain.reshape(16, LANES))
    column = exchanged(final_in, Z)
    rows = pl.pallas_call(
        spread_kernel,
        out_shape=shape((16, 8, width), bf16),
        in_specs=[VM],
        out_specs=VM,
        scratch_shapes=[pltpu.VMEM((8, 16, LANES), f32)],
        name="spread",
    )(column)
    near = exchanged(rows, (X, Y)).reshape(LANES, width)
    far = shifted(near, C, 1)
    near_logits, near_lse = pl.pallas_call(
        near_kernel,
        out_shape=(shape((LANES, vocab)), shape((8, LANES))),
        in_specs=[VM, VM],
        out_specs=(VM, VM),
        compiler_params=params(16),
        cost_estimate=cost(2 * 128 * 2048 * 512, 3 << 20),
        name="near_scores",
    )(near, vocab_weight)
    far_logits, lse = pl.pallas_call(
        far_kernel,
        out_shape=(shape((LANES, vocab)), shape((2, LANES))),
        in_specs=[VM, VM, VM],
        out_specs=(VM, VM),
        compiler_params=params(16),
        cost_estimate=cost(2 * 128 * 2048 * 512, 3 << 20),
        name="far_scores",
    )(far, vocab_weight, near_lse)
    other = shifted(lse, C, 1)
    chip = pl.pallas_call(
        chip_kernel,
        out_shape=shape((LANES, 2, LANES)),
        in_specs=[VM, VM],
        out_specs=VM,
        name="chip_total",
    )(lse, other)
    everyone = exchanged(chip, (Z, X, Y))
    log_probs = pl.pallas_call(
        score_kernel,
        out_shape=shape((16, TOKS, vocab)),
        in_specs=[VM] * 3,
        out_specs=VM,
        scratch_shapes=[pltpu.VMEM((8, LANES, LANES), f32)],
        compiler_params=params(8),
        name="log_probs",
    )(everyone, near_logits, far_logits)
    return (new_state[None, None, None], log_probs)


def solution(mesh):
    split = Mesh(
        mesh.devices.reshape(8, 2, mesh.shape["rows"], mesh.shape["heads"]),
        ALL,
    )
    return jax.shard_map(
        on_device,
        mesh=split,
        in_specs=(
            P(DP, None, None),
            P(),
            P(None, None, (Y, X)),
            P(None, None, (Y, X)),
            P(None, None, (Y, X)),
            P(None, None, (Y, X)),
            P(None, None, None, Y),
            P(None, Y),
            P(None, X),
            P(None, (Y, X), None),
            P(None, DP, Y, X, None),
            P(),
            P(None, ALL),
        ),
        out_specs=(P(None, DP, Y, X, None), P(None, None, ALL)),
        check_vma=False,
    )
```

```python
import jax
import jax.numpy as jnp
from jax import lax
from jax.experimental import pallas as pl
from jax.experimental.pallas import tpu as pltpu
from jax.sharding import Mesh
from jax.sharding import PartitionSpec as P

Z, C, X, Y = ("dp_0", "dp_1", "rows", "heads")
DP = (Z, C)
ALL = (Z, C, X, Y)

TOKS = 16
DK = 1024
LANES = 128
epsilon = 1e-06
f32, bf16 = jnp.float32, jnp.bfloat16
HIGHEST = lax.Precision.HIGHEST

VM = pl.BlockSpec(memory_space=pltpu.VMEM)
SM = pl.BlockSpec(memory_space=pltpu.SMEM)
HB = pl.BlockSpec(memory_space=pltpu.HBM)


def exchanged(parts, axes):
    return lax.all_to_all(parts, axes, 0, 0, tiled=True)


def shifted(shard, axis, step):
    size = lax.axis_size(axis)
    return lax.ppermute(shard, axis, [(i, (i + step) % size) for i in range(size)])


def in_hbm(*arrays):
    return [pltpu.with_memory_space_constraint(a, pltpu.HBM) for a in arrays]


def shape(dims, dtype=f32):
    return jax.ShapeDtypeStruct(dims, dtype)


def params(mib):
    return pltpu.CompilerParams(vmem_limit_bytes=mib << 20)


def cost(flops, size):
    return pl.CostEstimate(flops=flops, bytes_accessed=size, transcendentals=0)


def across(a, b):
    return lax.dot_general(
        a, b, (((1,), (1,)), ((), ())), precision=HIGHEST, preferred_element_type=f32
    )


def halves(a):
    high = a.astype(bf16)
    return high, (a - high.astype(f32)).astype(bf16)


def project_kernel(
    hidden, gain, key_w, query_w, value_w, state, own, sent, normed, key_out,
    hidden_v, gain_v, key_v, query_v, value_v, state_v, sems,
):
    pairs = (
        (hidden, hidden_v), (gain, gain_v), (key_w, key_v), (query_w, query_v),
        (state, state_v), (value_w, value_v),
    )
    copies = [pltpu.make_async_copy(a, b, sems.at[i]) for i, (a, b) in enumerate(pairs)]
    for copy in copies:
        copy.start()
    copies[0].wait()
    copies[1].wait()
    x = hidden_v[...].astype(f32)
    inverse = lax.rsqrt(jnp.mean(x * x, axis=-1, keepdims=True) + epsilon)
    inputs = (x * inverse * gain_v[...]).astype(bf16)
    normed[...] = inputs
    copies[2].wait()
    key = jnp.dot(inputs, key_v[...], preferred_element_type=f32)
    key_out[...] = key
    copies[3].wait()
    query = jnp.dot(inputs, query_v[...], preferred_element_type=f32)
    both = jnp.concatenate([key, query], axis=0)
    wide_key = jnp.concatenate([key, jnp.zeros((LANES - TOKS, key.shape[1]), f32)], axis=0)
    grams = across(both, wide_key)
    length = jnp.sum(query * query, axis=-1, keepdims=True)
    lane = lax.broadcasted_iota(jnp.int32, (TOKS, LANES), 1)
    grams = jnp.concatenate(
        [jnp.where(lane == TOKS, length, grams[:TOKS]), grams[TOKS:]], axis=1
    )
    own[TOKS:, DK:] = grams
    gram_high, gram_low = halves(grams)
    first = gram_high.astype(f32)
    second = pltpu.roll(gram_low.astype(f32), 64, 1)
    lane = lax.broadcasted_iota(jnp.int32, grams.shape, 1) % LANES
    grams = jnp.where(lane < 64, first, second).astype(bf16)
    high, low = halves(both)
    copies[4].wait()
    state_high, state_low = halves(state_v[...])
    first = jnp.dot(jnp.concatenate([high, low], axis=0), state_high, preferred_element_type=f32)
    second = jnp.dot(high, state_low, preferred_element_type=f32)
    lookups = first[: 2 * TOKS] + first[2 * TOKS :] + second
    own[:, :DK] = lookups
    sent[:, :DK] = lookups.astype(bf16)
    copies[5].wait()
    value = jnp.dot(inputs, value_v[...], preferred_element_type=f32)
    own[:TOKS, DK:] = value
    sent[:, DK:] = jnp.concatenate([value.astype(bf16), grams], axis=0)


def gate_kernel(normed, zgate_w, gate_w, rate, hidden, silu, aux, mine, wide):
    inputs = normed[...]
    z = jnp.dot(inputs, zgate_w[...], preferred_element_type=f32)
    silu[...] = z * jax.nn.sigmoid(z)
    inputs = inputs.astype(f32)
    gates = gate_w[...].astype(f32)
    decay_in = jnp.sum(inputs * gates[0:1], axis=-1, keepdims=True)
    strength = jax.nn.sigmoid(jnp.sum(inputs * gates[1:2], axis=-1, keepdims=True))
    softplus = jnp.maximum(decay_in, 0.0) + jnp.log1p(jnp.exp(-jnp.abs(decay_in)))
    decay = -rate[0, 0] * softplus
    t = lax.broadcasted_iota(jnp.int32, (TOKS, LANES), 0)
    j = lax.broadcasted_iota(jnp.int32, (TOKS, LANES), 1)
    decay_row = jnp.sum(jnp.where(t == j, decay, 0.0), axis=0, keepdims=True)
    log_col = jnp.sum(jnp.where(j <= t, decay_row, 0.0), axis=1, keepdims=True)
    log_row = jnp.sum(jnp.where(t <= j, decay, 0.0), axis=0, keepdims=True)
    causal = j <= t
    ratio = jnp.where(causal, jnp.exp(jnp.where(causal, log_col - log_row, 0.0)), 0.0)
    last = jnp.sum(decay, axis=0, keepdims=True)
    ones = jnp.ones((TOKS, LANES), f32)
    aux[0] = jnp.where(j < t, strength * ratio, 0.0)
    aux[1] = ratio
    aux[2] = strength * ones
    aux[3] = jnp.exp(log_col) * ones
    aux[4] = jnp.exp(last - log_col) * ones
    aux[5] = jnp.exp(last) * ones
    token = lax.axis_index(X) * lax.axis_size(Y) + lax.axis_index(Y)
    wide[...] = hidden[...].astype(f32)
    row = wide[pl.ds(token, 1), :]
    for k in range(16):
        mine[k : k + 1, :] = row[:, k * LANES : (k + 1) * LANES]


def solve_kernel(
    own, one, three, two, silu, aux, gain, out_w, message, updates, key_scale_out,
    values, reads,
):
    columns = silu.shape[1]
    place = lax.axis_index(X)
    for piece, step in ((own, 0), (one, 1), (three, 3), (two, 2)):
        source = lax.rem(place - step + 4, 4)
        part = piece[...].astype(f32)
        values[:, pl.ds(pl.multiple_of(source * columns, columns), columns)] = part[:TOKS, DK:]
        if step == 0:
            total, grams = part[:, :DK], part[TOKS:, DK:]
        else:
            coded = part[TOKS:, DK:]
            total = total + part[:, :DK]
            grams = grams + (coded + pltpu.roll(coded, grams.shape[1] - 64, 1))
    key_gram, cross_gram = grams[:, :LANES], grams[:, LANES:]
    t = lax.broadcasted_iota(jnp.int32, (TOKS, LANES), 0)
    j = lax.broadcasted_iota(jnp.int32, (TOKS, LANES), 1)
    diagonal = jnp.where(t == j, key_gram, 0.0)
    key_col = lax.rsqrt(jnp.sum(diagonal, axis=1, keepdims=True) + epsilon)
    key_row = lax.rsqrt(jnp.sum(diagonal, axis=0, keepdims=True) + epsilon)
    length = jnp.sum(jnp.where(j == TOKS, key_gram, 0.0), axis=1, keepdims=True)
    query_col = lax.rsqrt(length + epsilon) * DK ** (-0.5)
    key_scale_out[...] = key_col * jnp.ones((TOKS, LANES), f32)
    lower = aux[0] * key_gram * key_col * key_row
    mixing = aux[1] * cross_gram * query_col * key_row
    strength, grown, leftover = aux[2][:, :1], aux[3][:, :1], aux[4][:, :1]
    rest = strength * (values[...] - grown * (total[:TOKS] * key_col))
    readout = grown * (total[TOKS:] * query_col)
    solved = []
    for k in range(TOKS):
        update = rest[k : k + 1]
        solved.append(update)
        if k < TOKS - 1:
            rest = rest - lower[:, k : k + 1] * update
        readout = readout + mixing[:, k : k + 1] * update
    updates[...] = leftover * jnp.concatenate(solved, axis=0)
    reads[...] = readout
    inverse = lax.rsqrt(jnp.mean(readout * readout, axis=-1, keepdims=True) + epsilon)
    piece = reads[:, pl.ds(pl.multiple_of(place * columns, columns), columns)]
    gated = (piece * inverse * gain[...] * silu[...]).astype(bf16)
    partial = jnp.dot(gated, out_w[...], preferred_element_type=f32)
    for k in range(16):
        message[:, k, :] = partial[:, k * LANES : (k + 1) * LANES]


def final_kernel(parts, mine, gain, out):
    stream = mine[...] + jnp.sum(parts[...], axis=0)
    inverse = lax.rsqrt(jnp.sum(stream * stream, keepdims=True) / (16 * LANES) + epsilon)
    final = (stream * inverse * gain[...]).astype(bf16)
    for k in range(out.shape[0]):
        out[k] = final


def spread_kernel(column, out, wide):
    wide[...] = column[...].astype(f32)
    rows = jnp.concatenate([wide[:, k, :] for k in range(16)], axis=1).astype(bf16)
    for k in range(out.shape[0]):
        out[k] = rows


def near_kernel(inputs, vocab_w, logits, lse):
    result = jnp.dot(inputs[...], vocab_w[...], preferred_element_type=f32)
    logits[...] = result
    peak = jnp.max(result, axis=-1, keepdims=True)
    total = peak + jnp.log(jnp.sum(jnp.exp(result - peak), axis=-1, keepdims=True))
    lse[...] = jnp.transpose(jnp.broadcast_to(total, (LANES, LANES)))[:8]


def far_kernel(inputs, vocab_w, near_lse, logits, lse):
    result = jnp.dot(inputs[...], vocab_w[...], preferred_element_type=f32)
    logits[...] = result
    peak = jnp.max(result, axis=-1, keepdims=True)
    total = peak + jnp.log(jnp.sum(jnp.exp(result - peak), axis=-1, keepdims=True))
    lse[0:1] = near_lse[0:1]
    lse[1:2] = jnp.transpose(jnp.broadcast_to(total, (LANES, LANES)))[0:1]


def chip_kernel(mine, other, out):
    core = lax.axis_index(C)
    a = mine[...]
    b = jnp.concatenate([other[1:2], other[0:1]], axis=0)
    peak = jnp.maximum(a, b)
    both = peak + jnp.log(jnp.exp(a - peak) + jnp.exp(b - peak))
    both = jnp.where(core == 0, both, jnp.concatenate([both[1:2], both[0:1]], axis=0))
    out[...] = jnp.broadcast_to(both[None], out.shape)


def score_kernel(everyone, near, far, out, wide):
    core = lax.axis_index(C)
    parts = everyone[...]
    peak = jnp.max(parts, axis=0)
    total = peak + jnp.log(jnp.sum(jnp.exp(parts - peak[None]), axis=0))
    total = jnp.where(core == 0, total, jnp.concatenate([total[1:2], total[0:1]], axis=0))
    for k, logits in enumerate((near, far)):
        column = jnp.transpose(jnp.broadcast_to(total[k : k + 1], (LANES, LANES)))
        for m in range(logits.shape[1] // LANES):
            cut = slice(m * LANES, (m + 1) * LANES)
            wide[4 * k + m] = logits[:, cut] - column
        half = core if k == 0 else 1 - core
        for z in range(8):
            for m in range(logits.shape[1] // LANES):
                cut = slice(m * LANES, (m + 1) * LANES)
                out[2 * z + half, :, cut] = wide[4 * k + m, pl.ds(z, TOKS, stride=8), :]


def on_device(
    hidden,
    norm_gain,
    query_weight,
    key_weight,
    value_weight,
    zgate_weight,
    gate_weight,
    decay_rate,
    output_gain,
    output_weight,
    recurrent_state,
    final_gain,
    vocab_weight,
):
    hidden = hidden[0]
    width = hidden.shape[1]
    columns = query_weight.shape[2]
    state = recurrent_state[0, 0, 0]
    vocab = vocab_weight.shape[1]
    own, sent, normed, key = pl.pallas_call(
        project_kernel,
        out_shape=(
            shape((2 * TOKS, DK + columns)),
            shape((2 * TOKS, DK + columns), bf16),
            shape((TOKS, width), bf16),
            shape((TOKS, columns)),
        ),
        in_specs=[HB] * 6,
        out_specs=(VM, VM, VM, VM),
        scratch_shapes=[
            pltpu.VMEM((TOKS, width), bf16),
            pltpu.VMEM((1, width), f32),
            pltpu.VMEM((width, columns), bf16),
            pltpu.VMEM((width, columns), bf16),
            pltpu.VMEM((width, columns), bf16),
            pltpu.VMEM(state.shape, f32),
            pltpu.SemaphoreType.DMA((6,)),
        ],
        compiler_params=params(16),
        name="project",
    )(*in_hbm(hidden, norm_gain, key_weight[0], query_weight[0], value_weight[0], state))
    one, three, two = [shifted(sent, X, k) for k in (1, 3, 2)]
    silu, aux, mine = pl.pallas_call(
        gate_kernel,
        out_shape=(shape((TOKS, columns)), shape((6, TOKS, LANES)), shape((16, LANES))),
        in_specs=[VM, VM, VM, SM, VM],
        out_specs=(VM, VM, VM),
        scratch_shapes=[pltpu.VMEM((TOKS, width), f32)],
        compiler_params=params(8),
        cost_estimate=cost(16 * 2048 * 512, 1 << 21),
        name="gates",
    )(normed, zgate_weight[0], gate_weight[0, :, :, 0], decay_rate, hidden)
    message, updates, key_scale = pl.pallas_call(
        solve_kernel,
        out_shape=(
            shape((TOKS, 16, LANES)),
            shape((TOKS, DK)),
            shape((TOKS, LANES)),
        ),
        in_specs=[VM] * 8,
        out_specs=(VM, VM, VM),
        scratch_shapes=[pltpu.VMEM((TOKS, DK), f32), pltpu.VMEM((TOKS, DK), f32)],
        compiler_params=params(8),
        name="solve",
    )(own, one, three, two, silu, aux, output_gain, output_weight[0])
    parts = exchanged(message, (X, Y))
    final_in = pl.pallas_call(
        final_kernel,
        out_shape=shape((8, 16, LANES), bf16),
        in_specs=[VM] * 3,
        out_specs=VM,
        compiler_params=params(4),
        name="final_norm",
    )(parts, mine, final_gain.reshape(16, LANES))
    column = exchanged(final_in, Z)
    rows = pl.pallas_call(
        spread_kernel,
        out_shape=shape((16, 8, width), bf16),
        in_specs=[VM],
        out_specs=VM,
        scratch_shapes=[pltpu.VMEM((8, 16, LANES), f32)],
        compiler_params=params(4),
        name="spread",
    )(column)
    near = exchanged(rows, (X, Y)).reshape(LANES, width)
    far = shifted(near, C, 1)
    near_logits, near_lse = pl.pallas_call(
        near_kernel,
        out_shape=(shape((LANES, vocab)), shape((8, LANES))),
        in_specs=[VM, VM],
        out_specs=(VM, VM),
        compiler_params=params(16),
        cost_estimate=cost(2 * 128 * 2048 * 512, 3 << 20),
        name="near_scores",
    )(near, vocab_weight)
    far_logits, lse = pl.pallas_call(
        far_kernel,
        out_shape=(shape((LANES, vocab)), shape((2, LANES))),
        in_specs=[VM, VM, VM],
        out_specs=(VM, VM),
        compiler_params=params(16),
        cost_estimate=cost(2 * 128 * 2048 * 512, 3 << 20),
        name="far_scores",
    )(far, vocab_weight, near_lse)
    other = shifted(lse, C, 1)
    chip = pl.pallas_call(
        chip_kernel,
        out_shape=shape((LANES, 2, LANES)),
        in_specs=[VM, VM],
        out_specs=VM,
        compiler_params=params(4),
        name="chip_total",
    )(lse, other)
    chip, updates, key_scale, aux = lax.optimization_barrier((chip, updates, key_scale, aux))
    everyone = exchanged(chip, (Z, X, Y))
    new_state = aux[5, 0, 0] * state + jnp.dot(
        (key * key_scale[:, :1]).T, updates, precision=HIGHEST
    )
    log_probs = pl.pallas_call(
        score_kernel,
        out_shape=shape((16, TOKS, vocab)),
        in_specs=[VM] * 3,
        out_specs=VM,
        scratch_shapes=[pltpu.VMEM((8, LANES, LANES), f32)],
        compiler_params=params(8),
        name="log_probs",
    )(everyone, near_logits, far_logits)
    return (new_state[None, None, None], log_probs)


def solution(mesh):
    split = Mesh(
        mesh.devices.reshape(8, 2, mesh.shape["rows"], mesh.shape["heads"]),
        ALL,
    )
    return jax.shard_map(
        on_device,
        mesh=split,
        in_specs=(
            P(DP, None, None),
            P(),
            P(None, None, (Y, X)),
            P(None, None, (Y, X)),
            P(None, None, (Y, X)),
            P(None, None, (Y, X)),
            P(None, None, None, Y),
            P(None, Y),
            P(None, X),
            P(None, (Y, X), None),
            P(None, DP, Y, X, None),
            P(),
            P(None, ALL),
        ),
        out_specs=(P(None, DP, Y, X, None), P(None, None, ALL)),
        check_vma=False,
    )
```

```python
import jax
import jax.numpy as jnp
from jax import lax
from jax.experimental import pallas as pl
from jax.experimental.pallas import tpu as pltpu
from jax.sharding import Mesh
from jax.sharding import PartitionSpec as P

Z, C, X, Y = ("dp_0", "dp_1", "rows", "heads")
DP = (Z, C)
ALL = (Z, C, X, Y)

TOKS = 16
DK = 1024
LANES = 128
epsilon = 1e-06
f32, bf16 = jnp.float32, jnp.bfloat16
HIGHEST = lax.Precision.HIGHEST

VM = pl.BlockSpec(memory_space=pltpu.VMEM)
SM = pl.BlockSpec(memory_space=pltpu.SMEM)
HB = pl.BlockSpec(memory_space=pltpu.HBM)


def exchanged(parts, axes):
    return lax.all_to_all(parts, axes, 0, 0, tiled=True)


def shifted(shard, axis, step):
    size = lax.axis_size(axis)
    return lax.ppermute(shard, axis, [(i, (i + step) % size) for i in range(size)])


def in_hbm(*arrays):
    return [pltpu.with_memory_space_constraint(a, pltpu.HBM) for a in arrays]


def shape(dims, dtype=f32):
    return jax.ShapeDtypeStruct(dims, dtype)


def params(mib):
    return pltpu.CompilerParams(vmem_limit_bytes=mib << 20)


def cost(flops, size):
    return pl.CostEstimate(flops=flops, bytes_accessed=size, transcendentals=0)


def across(a, b):
    return lax.dot_general(
        a, b, (((1,), (1,)), ((), ())), precision=HIGHEST, preferred_element_type=f32
    )


def halves(a):
    high = a.astype(bf16)
    return high, (a - high.astype(f32)).astype(bf16)


def project_kernel(
    hidden, gain, key_w, query_w, value_w, state, own, sent, normed, key_out,
    hidden_v, gain_v, key_v, query_v, value_v, state_v, sems,
):
    pairs = (
        (hidden, hidden_v), (gain, gain_v), (key_w, key_v), (query_w, query_v),
        (state, state_v), (value_w, value_v),
    )
    copies = [pltpu.make_async_copy(a, b, sems.at[i]) for i, (a, b) in enumerate(pairs)]
    for copy in copies:
        copy.start()
    copies[0].wait()
    copies[1].wait()
    x = hidden_v[...].astype(f32)
    inverse = lax.rsqrt(jnp.mean(x * x, axis=-1, keepdims=True) + epsilon)
    inputs = (x * inverse * gain_v[...]).astype(bf16)
    normed[...] = inputs
    copies[2].wait()
    key = jnp.dot(inputs, key_v[...], preferred_element_type=f32)
    key_out[...] = key
    copies[3].wait()
    query = jnp.dot(inputs, query_v[...], preferred_element_type=f32)
    both = jnp.concatenate([key, query], axis=0)
    wide_key = jnp.concatenate([key, jnp.zeros((LANES - TOKS, key.shape[1]), f32)], axis=0)
    grams = across(both, wide_key)
    length = jnp.sum(query * query, axis=-1, keepdims=True)
    lane = lax.broadcasted_iota(jnp.int32, (TOKS, LANES), 1)
    grams = jnp.concatenate(
        [jnp.where(lane == TOKS, length, grams[:TOKS]), grams[TOKS:]], axis=1
    )
    own[TOKS:, DK:] = grams
    gram_high, gram_low = halves(grams)
    first = gram_high.astype(f32)
    second = pltpu.roll(gram_low.astype(f32), 64, 1)
    lane = lax.broadcasted_iota(jnp.int32, grams.shape, 1) % LANES
    grams = jnp.where(lane < 64, first, second).astype(bf16)
    high, low = halves(both)
    copies[4].wait()
    state_high, state_low = halves(state_v[...])
    first = jnp.dot(jnp.concatenate([high, low], axis=0), state_high, preferred_element_type=f32)
    second = jnp.dot(high, state_low, preferred_element_type=f32)
    lookups = first[: 2 * TOKS] + first[2 * TOKS :] + second
    own[:, :DK] = lookups
    sent[:, :DK] = lookups.astype(bf16)
    copies[5].wait()
    value = jnp.dot(inputs, value_v[...], preferred_element_type=f32)
    own[:TOKS, DK:] = value
    sent[:, DK:] = jnp.concatenate([value.astype(bf16), grams], axis=0)


def gate_kernel(normed, zgate_w, gate_w, rate, silu, aux):
    inputs = normed[...]
    z = jnp.dot(inputs, zgate_w[...], preferred_element_type=f32)
    silu[...] = z * jax.nn.sigmoid(z)
    inputs = inputs.astype(f32)
    gates = gate_w[...].astype(f32)
    decay_in = jnp.sum(inputs * gates[0:1], axis=-1, keepdims=True)
    strength = jax.nn.sigmoid(jnp.sum(inputs * gates[1:2], axis=-1, keepdims=True))
    softplus = jnp.maximum(decay_in, 0.0) + jnp.log1p(jnp.exp(-jnp.abs(decay_in)))
    decay = -rate[0, 0] * softplus
    t = lax.broadcasted_iota(jnp.int32, (TOKS, LANES), 0)
    j = lax.broadcasted_iota(jnp.int32, (TOKS, LANES), 1)
    decay_row = jnp.sum(jnp.where(t == j, decay, 0.0), axis=0, keepdims=True)
    log_col = jnp.sum(jnp.where(j <= t, decay_row, 0.0), axis=1, keepdims=True)
    log_row = jnp.sum(jnp.where(t <= j, decay, 0.0), axis=0, keepdims=True)
    causal = j <= t
    ratio = jnp.where(causal, jnp.exp(jnp.where(causal, log_col - log_row, 0.0)), 0.0)
    last = jnp.sum(decay, axis=0, keepdims=True)
    ones = jnp.ones((TOKS, LANES), f32)
    aux[0] = jnp.where(j < t, strength * ratio, 0.0)
    aux[1] = ratio
    aux[2] = strength * ones
    aux[3] = jnp.exp(log_col) * ones
    aux[4] = jnp.exp(last - log_col) * ones
    aux[5] = jnp.exp(last) * ones


def solve_kernel(
    own, one, three, two, silu, aux, gain, out_w, part, sent, updates, key_scale_out,
    values, reads,
):
    columns = silu.shape[1]
    place = lax.axis_index(X)
    for piece, step in ((own, 0), (one, 1), (three, 3), (two, 2)):
        source = lax.rem(place - step + 4, 4)
        held = piece[...].astype(f32)
        values[:, pl.ds(pl.multiple_of(source * columns, columns), columns)] = held[:TOKS, DK:]
        if step == 0:
            total, grams = held[:, :DK], held[TOKS:, DK:]
        else:
            coded = held[TOKS:, DK:]
            total = total + held[:, :DK]
            grams = grams + (coded + pltpu.roll(coded, grams.shape[1] - 64, 1))
    key_gram, cross_gram = grams[:, :LANES], grams[:, LANES:]
    t = lax.broadcasted_iota(jnp.int32, (TOKS, LANES), 0)
    j = lax.broadcasted_iota(jnp.int32, (TOKS, LANES), 1)
    diagonal = jnp.where(t == j, key_gram, 0.0)
    key_col = lax.rsqrt(jnp.sum(diagonal, axis=1, keepdims=True) + epsilon)
    key_row = lax.rsqrt(jnp.sum(diagonal, axis=0, keepdims=True) + epsilon)
    length = jnp.sum(jnp.where(j == TOKS, key_gram, 0.0), axis=1, keepdims=True)
    query_col = lax.rsqrt(length + epsilon) * DK ** (-0.5)
    key_scale_out[...] = key_col * jnp.ones((TOKS, LANES), f32)
    lower = aux[0] * key_gram * key_col * key_row
    mixing = aux[1] * cross_gram * query_col * key_row
    strength, grown, leftover = aux[2][:, :1], aux[3][:, :1], aux[4][:, :1]
    rest = strength * (values[...] - grown * (total[:TOKS] * key_col))
    readout = grown * (total[TOKS:] * query_col)
    solved = []
    for k in range(TOKS):
        update = rest[k : k + 1]
        solved.append(update)
        if k < TOKS - 1:
            rest = rest - lower[:, k : k + 1] * update
        readout = readout + mixing[:, k : k + 1] * update
    updates[...] = leftover * jnp.concatenate(solved, axis=0)
    reads[...] = readout
    inverse = lax.rsqrt(jnp.mean(readout * readout, axis=-1, keepdims=True) + epsilon)
    piece = reads[:, pl.ds(pl.multiple_of(place * columns, columns), columns)]
    gated = (piece * inverse * gain[...] * silu[...]).astype(bf16)
    partial = jnp.dot(gated, out_w[...], preferred_element_type=f32)
    part[...] = partial
    sent[...] = partial.astype(bf16)


def state_kernel(state, key, key_scale, updates, aux, out):
    normalized = key[...] * key_scale[:, :1]
    added = lax.dot_general(
        normalized, updates[...], (((0,), (0,)), ((), ())), precision=HIGHEST,
        preferred_element_type=f32,
    )
    out[...] = aux[5][:1, :1] * state[...] + added


def rows_sum_kernel(part, one, three, two, total, sent):
    result = (part[...] + two[...].astype(f32)) + (one[...].astype(f32) + three[...].astype(f32))
    total[...] = result
    sent[...] = result.astype(bf16)


def final_kernel(total, one, three, two, hidden, gain, out):
    layer = (total[...] + two[...].astype(f32)) + (one[...].astype(f32) + three[...].astype(f32))
    stream = hidden[...].astype(f32) + layer
    inverse = lax.rsqrt(jnp.mean(stream * stream, axis=-1, keepdims=True) + epsilon)
    final = (stream * inverse * gain[...]).astype(bf16)
    for k in range(out.shape[0]):
        out[k] = final


def near_kernel(inputs, vocab_w, logits, lse):
    result = jnp.dot(inputs[...], vocab_w[...], preferred_element_type=f32)
    logits[...] = result
    peak = jnp.max(result, axis=-1, keepdims=True)
    total = peak + jnp.log(jnp.sum(jnp.exp(result - peak), axis=-1, keepdims=True))
    lse[...] = jnp.transpose(jnp.broadcast_to(total, (LANES, LANES)))[:8]


def far_kernel(inputs, vocab_w, near_lse, logits, lse):
    result = jnp.dot(inputs[...], vocab_w[...], preferred_element_type=f32)
    logits[...] = result
    peak = jnp.max(result, axis=-1, keepdims=True)
    total = peak + jnp.log(jnp.sum(jnp.exp(result - peak), axis=-1, keepdims=True))
    lse[0:1] = near_lse[0:1]
    lse[1:2] = jnp.transpose(jnp.broadcast_to(total, (LANES, LANES)))[0:1]


def chip_kernel(mine, other, out):
    core = lax.axis_index(C)
    a = mine[...]
    b = jnp.concatenate([other[1:2], other[0:1]], axis=0)
    peak = jnp.maximum(a, b)
    both = peak + jnp.log(jnp.exp(a - peak) + jnp.exp(b - peak))
    both = jnp.where(core == 0, both, jnp.concatenate([both[1:2], both[0:1]], axis=0))
    out[...] = jnp.broadcast_to(both[None], out.shape)


def score_kernel(everyone, near, far, out):
    core = lax.axis_index(C)
    parts = everyone[...]
    peak = jnp.max(parts, axis=0)
    total = peak + jnp.log(jnp.sum(jnp.exp(parts - peak[None]), axis=0))
    total = jnp.where(core == 0, total, jnp.concatenate([total[1:2], total[0:1]], axis=0))
    for k, logits in enumerate((near, far)):
        column = jnp.transpose(jnp.broadcast_to(total[k : k + 1], (LANES, LANES)))[:, :1]
        half = core if k == 0 else 1 - core
        for z in range(8):
            cut = slice(z * TOKS, (z + 1) * TOKS)
            out[2 * z + half] = logits[cut] - column[cut]


def on_device(
    hidden,
    norm_gain,
    query_weight,
    key_weight,
    value_weight,
    zgate_weight,
    gate_weight,
    decay_rate,
    output_gain,
    output_weight,
    recurrent_state,
    final_gain,
    vocab_weight,
):
    hidden = hidden[0]
    width = hidden.shape[1]
    columns = query_weight.shape[2]
    state = recurrent_state[0, 0, 0]
    vocab = vocab_weight.shape[1]
    own, sent, normed, key = pl.pallas_call(
        project_kernel,
        out_shape=(
            shape((2 * TOKS, DK + columns)),
            shape((2 * TOKS, DK + columns), bf16),
            shape((TOKS, width), bf16),
            shape((TOKS, columns)),
        ),
        in_specs=[HB] * 6,
        out_specs=(VM, VM, VM, VM),
        scratch_shapes=[
            pltpu.VMEM((TOKS, width), bf16),
            pltpu.VMEM((1, width), f32),
            pltpu.VMEM((width, columns), bf16),
            pltpu.VMEM((width, columns), bf16),
            pltpu.VMEM((width, columns), bf16),
            pltpu.VMEM(state.shape, f32),
            pltpu.SemaphoreType.DMA((6,)),
        ],
        compiler_params=params(16),
        name="project",
    )(*in_hbm(hidden, norm_gain, key_weight[0], query_weight[0], value_weight[0], state))
    one, three, two = [shifted(sent, X, k) for k in (1, 3, 2)]
    silu, aux = pl.pallas_call(
        gate_kernel,
        out_shape=(shape((TOKS, columns)), shape((6, TOKS, LANES))),
        in_specs=[VM, VM, VM, SM],
        out_specs=(VM, VM),
        compiler_params=params(8),
        cost_estimate=cost(16 * 2048 * 512, 1 << 21),
        name="gates",
    )(normed, zgate_weight[0], gate_weight[0, :, :, 0], decay_rate)
    part, sent, updates, key_scale = pl.pallas_call(
        solve_kernel,
        out_shape=(
            shape((TOKS, width)),
            shape((TOKS, width), bf16),
            shape((TOKS, DK)),
            shape((TOKS, LANES)),
        ),
        in_specs=[VM] * 8,
        out_specs=(VM,) * 4,
        scratch_shapes=[pltpu.VMEM((TOKS, DK), f32), pltpu.VMEM((TOKS, DK), f32)],
        compiler_params=params(8),
        name="solve",
    )(own, one, three, two, silu, aux, output_gain, output_weight[0])
    one, three, two = [shifted(sent, X, k) for k in (1, 3, 2)]
    new_state = pl.pallas_call(
        state_kernel,
        out_shape=shape(state.shape),
        in_specs=[VM] * 5,
        out_specs=VM,
        compiler_params=params(8),
        cost_estimate=cost(2 * 16 * 256 * 1024 * 6, 2 << 20),
        name="next_state",
    )(state, key, key_scale, updates, aux)
    one, three, two, new_state = lax.optimization_barrier((one, three, two, new_state))
    total, sent = pl.pallas_call(
        rows_sum_kernel,
        out_shape=(shape((TOKS, width)), shape((TOKS, width), bf16)),
        in_specs=[VM] * 4,
        out_specs=(VM, VM),
        compiler_params=params(4),
        name="rows_sum",
    )(part, one, three, two)
    one, three, two = [shifted(sent, Y, k) for k in (1, 3, 2)]
    final_in = pl.pallas_call(
        final_kernel,
        out_shape=shape((8, TOKS, width), bf16),
        in_specs=[VM] * 6,
        out_specs=VM,
        compiler_params=params(4),
        name="final_norm",
    )(total, one, three, two, hidden, final_gain[None])
    near = exchanged(final_in, Z).reshape(LANES, width)
    far = shifted(near, C, 1)
    near_logits, near_lse = pl.pallas_call(
        near_kernel,
        out_shape=(shape((LANES, vocab)), shape((8, LANES))),
        in_specs=[VM, VM],
        out_specs=(VM, VM),
        compiler_params=params(16),
        cost_estimate=cost(2 * 128 * 2048 * 512, 3 << 20),
        name="near_scores",
    )(near, vocab_weight)
    far_logits, lse = pl.pallas_call(
        far_kernel,
        out_shape=(shape((LANES, vocab)), shape((2, LANES))),
        in_specs=[VM, VM, VM],
        out_specs=(VM, VM),
        compiler_params=params(16),
        cost_estimate=cost(2 * 128 * 2048 * 512, 3 << 20),
        name="far_scores",
    )(far, vocab_weight, near_lse)
    other = shifted(lse, C, 1)
    chip = pl.pallas_call(
        chip_kernel,
        out_shape=shape((LANES, 2, LANES)),
        in_specs=[VM, VM],
        out_specs=VM,
        compiler_params=params(4),
        name="chip_total",
    )(lse, other)
    everyone = exchanged(chip, (Z, X, Y))
    log_probs = pl.pallas_call(
        score_kernel,
        out_shape=shape((16, TOKS, vocab)),
        in_specs=[VM] * 3,
        out_specs=VM,
        compiler_params=params(8),
        name="log_probs",
    )(everyone, near_logits, far_logits)
    return (new_state[None, None, None], log_probs)


def solution(mesh):
    split = Mesh(
        mesh.devices.reshape(8, 2, mesh.shape["rows"], mesh.shape["heads"]),
        ALL,
    )
    return jax.shard_map(
        on_device,
        mesh=split,
        in_specs=(
            P(DP, None, None),
            P(),
            P(None, None, (Y, X)),
            P(None, None, (Y, X)),
            P(None, None, (Y, X)),
            P(None, None, (Y, X)),
            P(None, None, None, Y),
            P(None, Y),
            P(None, X),
            P(None, (Y, X), None),
            P(None, DP, Y, X, None),
            P(),
            P(None, ALL),
        ),
        out_specs=(P(None, DP, Y, X, None), P(None, None, ALL)),
        check_vma=False,
    )
```

```python
import jax
import jax.numpy as jnp
from jax import lax
from jax.experimental import pallas as pl
from jax.experimental.pallas import tpu as pltpu
from jax.sharding import Mesh
from jax.sharding import PartitionSpec as P

Z, C, X, Y = ("dp_0", "dp_1", "rows", "heads")
DP = (Z, C)
ALL = (Z, C, X, Y)

TOKS = 16
DK = 1024
LANES = 128
epsilon = 1e-06
f32, bf16 = jnp.float32, jnp.bfloat16
HIGHEST = lax.Precision.HIGHEST

VM = pl.BlockSpec(memory_space=pltpu.VMEM)
SM = pl.BlockSpec(memory_space=pltpu.SMEM)
HB = pl.BlockSpec(memory_space=pltpu.HBM)


def exchanged(parts, axes):
    return lax.all_to_all(parts, axes, 0, 0, tiled=True)


def swapped(shard, axis, step):
    return lax.ppermute(shard, axis, [(i, i ^ step) for i in range(lax.axis_size(axis))])


def in_hbm(*arrays):
    return [pltpu.with_memory_space_constraint(a, pltpu.HBM) for a in arrays]


def shape(dims, dtype=f32):
    return jax.ShapeDtypeStruct(dims, dtype)


def params(mib):
    return pltpu.CompilerParams(vmem_limit_bytes=mib << 20)


def cost(flops, size):
    return pl.CostEstimate(flops=flops, bytes_accessed=size, transcendentals=0)


def across(a, b):
    return lax.dot_general(
        a, b, (((1,), (1,)), ((), ())), precision=HIGHEST, preferred_element_type=f32
    )


def halves(a):
    high = a.astype(bf16)
    return high, (a - high.astype(f32)).astype(bf16)


def project_kernel(
    hidden, gain, key_w, query_w, value_w, state, own, sent, normed, key_out,
    hidden_v, gain_v, key_v, query_v, value_v, state_v, sems,
):
    pairs = (
        (hidden, hidden_v), (gain, gain_v), (key_w, key_v), (query_w, query_v),
        (state, state_v), (value_w, value_v),
    )
    copies = [pltpu.make_async_copy(a, b, sems.at[i]) for i, (a, b) in enumerate(pairs)]
    for copy in copies:
        copy.start()
    copies[0].wait()
    copies[1].wait()
    x = hidden_v[...].astype(f32)
    inverse = lax.rsqrt(jnp.mean(x * x, axis=-1, keepdims=True) + epsilon)
    inputs = (x * inverse * gain_v[...]).astype(bf16)
    normed[...] = inputs
    copies[2].wait()
    key = jnp.dot(inputs, key_v[...], preferred_element_type=f32)
    key_out[...] = key
    copies[3].wait()
    query = jnp.dot(inputs, query_v[...], preferred_element_type=f32)
    both = jnp.concatenate([key, query], axis=0)
    wide_key = jnp.concatenate([key, jnp.zeros((LANES - TOKS, key.shape[1]), f32)], axis=0)
    grams = across(both, wide_key)
    length = jnp.sum(query * query, axis=-1, keepdims=True)
    lane = lax.broadcasted_iota(jnp.int32, (TOKS, LANES), 1)
    grams = jnp.concatenate(
        [jnp.where(lane == TOKS, length, grams[:TOKS]), grams[TOKS:]], axis=1
    )
    own[TOKS:, DK:] = grams
    gram_high, gram_low = halves(grams)
    first = gram_high.astype(f32)
    second = pltpu.roll(gram_low.astype(f32), 64, 1)
    lane = lax.broadcasted_iota(jnp.int32, grams.shape, 1) % LANES
    grams = jnp.where(lane < 64, first, second).astype(bf16)
    high, low = halves(both)
    copies[4].wait()
    state_high, state_low = halves(state_v[...])
    first = jnp.dot(jnp.concatenate([high, low], axis=0), state_high, preferred_element_type=f32)
    second = jnp.dot(high, state_low, preferred_element_type=f32)
    lookups = first[: 2 * TOKS] + first[2 * TOKS :] + second
    own[:, :DK] = lookups
    sent[:, :DK] = lookups.astype(bf16)
    copies[5].wait()
    value = jnp.dot(inputs, value_v[...], preferred_element_type=f32)
    own[:TOKS, DK:] = value
    sent[:, DK:] = jnp.concatenate([value.astype(bf16), grams], axis=0)


def gate_kernel(normed, zgate_w, gate_w, rate, silu, aux):
    inputs = normed[...]
    z = jnp.dot(inputs, zgate_w[...], preferred_element_type=f32)
    silu[...] = z * jax.nn.sigmoid(z)
    inputs = inputs.astype(f32)
    gates = gate_w[...].astype(f32)
    decay_in = jnp.sum(inputs * gates[0:1], axis=-1, keepdims=True)
    strength = jax.nn.sigmoid(jnp.sum(inputs * gates[1:2], axis=-1, keepdims=True))
    softplus = jnp.maximum(decay_in, 0.0) + jnp.log1p(jnp.exp(-jnp.abs(decay_in)))
    decay = -rate[0, 0] * softplus
    t = lax.broadcasted_iota(jnp.int32, (TOKS, LANES), 0)
    j = lax.broadcasted_iota(jnp.int32, (TOKS, LANES), 1)
    decay_row = jnp.sum(jnp.where(t == j, decay, 0.0), axis=0, keepdims=True)
    log_col = jnp.sum(jnp.where(j <= t, decay_row, 0.0), axis=1, keepdims=True)
    log_row = jnp.sum(jnp.where(t <= j, decay, 0.0), axis=0, keepdims=True)
    causal = j <= t
    ratio = jnp.where(causal, jnp.exp(jnp.where(causal, log_col - log_row, 0.0)), 0.0)
    last = jnp.sum(decay, axis=0, keepdims=True)
    ones = jnp.ones((TOKS, LANES), f32)
    aux[0] = jnp.where(j < t, strength * ratio, 0.0)
    aux[1] = ratio
    aux[2] = strength * ones
    aux[3] = jnp.exp(log_col) * ones
    aux[4] = jnp.exp(last - log_col) * ones
    aux[5] = jnp.exp(last) * ones


def solve_kernel(
    own, one, three, two, silu, aux, gain, out_w, part, sent, updates, key_scale_out,
    values, reads,
):
    columns = silu.shape[1]
    place = lax.axis_index(X)
    for piece, step in ((own, 0), (one, 1), (three, 3), (two, 2)):
        source = place ^ step
        held = piece[...].astype(f32)
        values[:, pl.ds(pl.multiple_of(source * columns, columns), columns)] = held[:TOKS, DK:]
        if step == 0:
            total, grams = held[:, :DK], held[TOKS:, DK:]
        else:
            coded = held[TOKS:, DK:]
            total = total + held[:, :DK]
            grams = grams + (coded + pltpu.roll(coded, grams.shape[1] - 64, 1))
    key_gram, cross_gram = grams[:, :LANES], grams[:, LANES:]
    t = lax.broadcasted_iota(jnp.int32, (TOKS, LANES), 0)
    j = lax.broadcasted_iota(jnp.int32, (TOKS, LANES), 1)
    diagonal = jnp.where(t == j, key_gram, 0.0)
    key_col = lax.rsqrt(jnp.sum(diagonal, axis=1, keepdims=True) + epsilon)
    key_row = lax.rsqrt(jnp.sum(diagonal, axis=0, keepdims=True) + epsilon)
    length = jnp.sum(jnp.where(j == TOKS, key_gram, 0.0), axis=1, keepdims=True)
    query_col = lax.rsqrt(length + epsilon) * DK ** (-0.5)
    key_scale_out[...] = key_col * jnp.ones((TOKS, LANES), f32)
    lower = aux[0] * key_gram * key_col * key_row
    mixing = aux[1] * cross_gram * query_col * key_row
    strength, grown, leftover = aux[2][:, :1], aux[3][:, :1], aux[4][:, :1]
    rest = strength * (values[...] - grown * (total[:TOKS] * key_col))
    readout = grown * (total[TOKS:] * query_col)
    solved = []
    for k in range(TOKS):
        update = rest[k : k + 1]
        solved.append(update)
        if k < TOKS - 1:
            rest = rest - lower[:, k : k + 1] * update
        readout = readout + mixing[:, k : k + 1] * update
    updates[...] = leftover * jnp.concatenate(solved, axis=0)
    reads[...] = readout
    inverse = lax.rsqrt(jnp.mean(readout * readout, axis=-1, keepdims=True) + epsilon)
    piece = reads[:, pl.ds(pl.multiple_of(place * columns, columns), columns)]
    gated = (piece * inverse * gain[...] * silu[...]).astype(bf16)
    partial = jnp.dot(gated, out_w[...], preferred_element_type=f32)
    part[...] = partial
    sent[...] = partial.astype(bf16)


def state_kernel(state, key, key_scale, updates, aux, out):
    normalized = key[...] * key_scale[:, :1]
    added = lax.dot_general(
        normalized, updates[...], (((0,), (0,)), ((), ())), precision=HIGHEST,
        preferred_element_type=f32,
    )
    out[...] = aux[5][:1, :1] * state[...] + added


def rows_sum_kernel(part, one, three, two, total, sent):
    result = (part[...] + two[...].astype(f32)) + (one[...].astype(f32) + three[...].astype(f32))
    total[...] = result
    sent[...] = result.astype(bf16)


def final_kernel(total, one, three, two, hidden, gain, out):
    layer = (total[...] + two[...].astype(f32)) + (one[...].astype(f32) + three[...].astype(f32))
    stream = hidden[...].astype(f32) + layer
    inverse = lax.rsqrt(jnp.mean(stream * stream, axis=-1, keepdims=True) + epsilon)
    final = (stream * inverse * gain[...]).astype(bf16)
    for k in range(out.shape[0]):
        out[k] = final


def near_kernel(inputs, vocab_w, logits, lse):
    result = jnp.dot(inputs[...], vocab_w[...], preferred_element_type=f32)
    logits[...] = result
    lse[...] = log_sum_exp(result)


def far_kernel(inputs, vocab_w, other, logits, chip):
    result = jnp.dot(inputs[...], vocab_w[...], preferred_element_type=f32)
    logits[...] = result
    a, b = log_sum_exp(result), other[...]
    peak = jnp.maximum(a, b)
    both = peak + jnp.log(jnp.exp(a - peak) + jnp.exp(b - peak))
    chip[...] = jnp.broadcast_to(both, chip.shape)


def log_sum_exp(logits):
    peak = jnp.max(logits, axis=-1, keepdims=True)
    total = peak + jnp.log(jnp.sum(jnp.exp(logits - peak), axis=-1, keepdims=True))
    return jnp.transpose(jnp.broadcast_to(total, (LANES, LANES)))[0:1]


def total_kernel(everyone, total):
    parts = everyone[...]
    peak = jnp.max(parts, axis=0, keepdims=True)
    total[...] = peak + jnp.log(jnp.sum(jnp.exp(parts - peak), axis=0, keepdims=True))


def score_kernel(far_total, near_total, far, near, out, wide, sems):
    core = lax.axis_index(C)
    copies = []
    for k, (logits, total) in enumerate(((far, far_total), (near, near_total))):
        half = 1 - core if k == 0 else core
        column = jnp.transpose(jnp.broadcast_to(total[...], (LANES, LANES)))[:, :1]
        for z in range(8):
            cut = slice(z * TOKS, (z + 1) * TOKS)
            wide[k, z] = logits[cut] - column[cut]
        for z in range(8):
            copies.append(
                pltpu.make_async_copy(wide.at[k, z], out.at[2 * z + half], sems.at[k, z])
            )
            copies[-1].start()
    for copy in copies:
        copy.wait()


def on_device(
    hidden,
    norm_gain,
    query_weight,
    key_weight,
    value_weight,
    zgate_weight,
    gate_weight,
    decay_rate,
    output_gain,
    output_weight,
    recurrent_state,
    final_gain,
    vocab_weight,
):
    hidden = hidden[0]
    width = hidden.shape[1]
    columns = query_weight.shape[2]
    state = recurrent_state[0, 0, 0]
    vocab = vocab_weight.shape[1]
    own, sent, normed, key = pl.pallas_call(
        project_kernel,
        out_shape=(
            shape((2 * TOKS, DK + columns)),
            shape((2 * TOKS, DK + columns), bf16),
            shape((TOKS, width), bf16),
            shape((TOKS, columns)),
        ),
        in_specs=[HB] * 6,
        out_specs=(VM, VM, VM, VM),
        scratch_shapes=[
            pltpu.VMEM((TOKS, width), bf16),
            pltpu.VMEM((1, width), f32),
            pltpu.VMEM((width, columns), bf16),
            pltpu.VMEM((width, columns), bf16),
            pltpu.VMEM((width, columns), bf16),
            pltpu.VMEM(state.shape, f32),
            pltpu.SemaphoreType.DMA((6,)),
        ],
        compiler_params=params(16),
        name="project",
    )(*in_hbm(hidden, norm_gain, key_weight[0], query_weight[0], value_weight[0], state))
    one, three, two = [swapped(sent, X, k) for k in (1, 3, 2)]
    silu, aux = pl.pallas_call(
        gate_kernel,
        out_shape=(shape((TOKS, columns)), shape((6, TOKS, LANES))),
        in_specs=[VM, VM, VM, SM],
        out_specs=(VM, VM),
        compiler_params=params(8),
        cost_estimate=cost(16 * 2048 * 512, 1 << 21),
        name="gates",
    )(normed, zgate_weight[0], gate_weight[0, :, :, 0], decay_rate)
    part, sent, updates, key_scale = pl.pallas_call(
        solve_kernel,
        out_shape=(
            shape((TOKS, width)),
            shape((TOKS, width), bf16),
            shape((TOKS, DK)),
            shape((TOKS, LANES)),
        ),
        in_specs=[VM] * 8,
        out_specs=(VM,) * 4,
        scratch_shapes=[pltpu.VMEM((TOKS, DK), f32), pltpu.VMEM((TOKS, DK), f32)],
        compiler_params=params(8),
        name="solve",
    )(own, one, three, two, silu, aux, output_gain, output_weight[0])
    one, three, two = [swapped(sent, X, k) for k in (1, 3, 2)]
    new_state = pl.pallas_call(
        state_kernel,
        out_shape=shape(state.shape),
        in_specs=[VM] * 5,
        out_specs=VM,
        compiler_params=params(8),
        cost_estimate=cost(2 * 16 * 256 * 1024 * 6, 2 << 20),
        name="next_state",
    )(state, key, key_scale, updates, aux)
    one, three, two, new_state = lax.optimization_barrier((one, three, two, new_state))
    total, sent = pl.pallas_call(
        rows_sum_kernel,
        out_shape=(shape((TOKS, width)), shape((TOKS, width), bf16)),
        in_specs=[VM] * 4,
        out_specs=(VM, VM),
        compiler_params=params(4),
        name="rows_sum",
    )(part, one, three, two)
    one, three, two = [swapped(sent, Y, k) for k in (1, 3, 2)]
    final_in = pl.pallas_call(
        final_kernel,
        out_shape=shape((8, TOKS, width), bf16),
        in_specs=[VM] * 6,
        out_specs=VM,
        compiler_params=params(4),
        name="final_norm",
    )(total, one, three, two, hidden, final_gain[None])
    near = exchanged(final_in, Z).reshape(LANES, width)
    far = swapped(near, C, 1)
    near_logits, lse = pl.pallas_call(
        near_kernel,
        out_shape=(shape((LANES, vocab)), shape((1, LANES))),
        in_specs=[VM, VM],
        out_specs=(VM, VM),
        compiler_params=params(8),
        cost_estimate=cost(2 * 128 * 2048 * 512, 3 << 20),
        name="near_scores",
    )(near, vocab_weight)
    other = swapped(lse, C, 1)
    far_logits, chip = pl.pallas_call(
        far_kernel,
        out_shape=(shape((LANES, vocab)), shape((LANES, LANES))),
        in_specs=[VM, VM, VM],
        out_specs=(VM, VM),
        compiler_params=params(8),
        cost_estimate=cost(2 * 128 * 2048 * 512, 3 << 20),
        name="far_scores",
    )(far, vocab_weight, other)
    everyone = exchanged(chip, (Z, X, Y))
    far_total = pl.pallas_call(
        total_kernel,
        out_shape=shape((1, LANES)),
        in_specs=[VM],
        out_specs=VM,
        compiler_params=params(4),
        name="total",
    )(everyone)
    near_total = swapped(far_total, C, 1)
    log_probs = pl.pallas_call(
        score_kernel,
        out_shape=shape((16, TOKS, vocab)),
        in_specs=[VM] * 4,
        out_specs=HB,
        scratch_shapes=[
            pltpu.VMEM((2, 8, TOKS, vocab), f32),
            pltpu.SemaphoreType.DMA((2, 8)),
        ],
        compiler_params=params(8),
        name="log_probs",
    )(far_total, near_total, far_logits, near_logits)
    return (new_state[None, None, None], log_probs)


def solution(mesh):
    split = Mesh(
        mesh.devices.reshape(8, 2, mesh.shape["rows"], mesh.shape["heads"]),
        ALL,
    )
    return jax.shard_map(
        on_device,
        mesh=split,
        in_specs=(
            P(DP, None, None),
            P(),
            P(None, None, (Y, X)),
            P(None, None, (Y, X)),
            P(None, None, (Y, X)),
            P(None, None, (Y, X)),
            P(None, None, None, Y),
            P(None, Y),
            P(None, X),
            P(None, (Y, X), None),
            P(None, DP, Y, X, None),
            P(),
            P(None, ALL),
        ),
        out_specs=(P(None, DP, Y, X, None), P(None, None, ALL)),
        check_vma=False,
    )
```

```python
import jax
import jax.numpy as jnp
from jax import lax
from jax.experimental import pallas as pl
from jax.experimental.pallas import tpu as pltpu
from jax.sharding import Mesh
from jax.sharding import PartitionSpec as P

Z, C, X, Y = ("dp_0", "dp_1", "rows", "heads")
DP = (Z, C)
ALL = (Z, C, X, Y)

TOKS = 16
DK = 1024
LANES = 128
epsilon = 1e-06
f32, bf16 = jnp.float32, jnp.bfloat16
HIGHEST = lax.Precision.HIGHEST

VM = pl.BlockSpec(memory_space=pltpu.VMEM)
SM = pl.BlockSpec(memory_space=pltpu.SMEM)
HB = pl.BlockSpec(memory_space=pltpu.HBM)


def exchanged(parts, axes):
    return lax.all_to_all(parts, axes, 0, 0, tiled=True)


def swapped(shard, axes, step):
    return lax.ppermute(shard, axes, [(i, i ^ step) for i in range(lax.axis_size(axes))])


def in_hbm(*arrays):
    return [pltpu.with_memory_space_constraint(a, pltpu.HBM) for a in arrays]


def shape(dims, dtype=f32):
    return jax.ShapeDtypeStruct(dims, dtype)


def params(mib):
    return pltpu.CompilerParams(vmem_limit_bytes=mib << 20)


def cost(flops, size):
    return pl.CostEstimate(flops=flops, bytes_accessed=size, transcendentals=0)


def across(a, b):
    return lax.dot_general(
        a, b, (((1,), (1,)), ((), ())), precision=HIGHEST, preferred_element_type=f32
    )


def halves(a):
    high = a.astype(bf16)
    return high, (a - high.astype(f32)).astype(bf16)


def project_kernel(
    hidden, gain, key_w, query_w, value_w, state, own, sent, normed, key_out,
    hidden_v, gain_v, key_v, query_v, value_v, state_v, sems,
):
    pairs = (
        (hidden, hidden_v), (gain, gain_v), (key_w, key_v), (query_w, query_v),
        (state, state_v), (value_w, value_v),
    )
    copies = [pltpu.make_async_copy(a, b, sems.at[i]) for i, (a, b) in enumerate(pairs)]
    for copy in copies:
        copy.start()
    copies[0].wait()
    copies[1].wait()
    x = hidden_v[...].astype(f32)
    inverse = lax.rsqrt(jnp.mean(x * x, axis=-1, keepdims=True) + epsilon)
    inputs = (x * inverse * gain_v[...]).astype(bf16)
    normed[...] = inputs
    copies[2].wait()
    key = jnp.dot(inputs, key_v[...], preferred_element_type=f32)
    key_out[...] = key
    copies[3].wait()
    query = jnp.dot(inputs, query_v[...], preferred_element_type=f32)
    both = jnp.concatenate([key, query], axis=0)
    wide_key = jnp.concatenate([key, jnp.zeros((LANES - TOKS, key.shape[1]), f32)], axis=0)
    grams = across(both, wide_key)
    length = jnp.sum(query * query, axis=-1, keepdims=True)
    lane = lax.broadcasted_iota(jnp.int32, (TOKS, LANES), 1)
    grams = jnp.concatenate(
        [jnp.where(lane == TOKS, length, grams[:TOKS]), grams[TOKS:]], axis=1
    )
    own[TOKS:, DK:] = grams
    gram_high, gram_low = halves(grams)
    first = gram_high.astype(f32)
    second = pltpu.roll(gram_low.astype(f32), 64, 1)
    lane = lax.broadcasted_iota(jnp.int32, grams.shape, 1) % LANES
    grams = jnp.where(lane < 64, first, second).astype(bf16)
    high, low = halves(both)
    copies[4].wait()
    state_high, state_low = halves(state_v[...])
    first = jnp.dot(jnp.concatenate([high, low], axis=0), state_high, preferred_element_type=f32)
    second = jnp.dot(high, state_low, preferred_element_type=f32)
    lookups = first[: 2 * TOKS] + first[2 * TOKS :] + second
    own[:, :DK] = lookups
    sent[:, :DK] = lookups.astype(bf16)
    copies[5].wait()
    value = jnp.dot(inputs, value_v[...], preferred_element_type=f32)
    own[:TOKS, DK:] = value
    sent[:, DK:] = jnp.concatenate([value.astype(bf16), grams], axis=0)


def gate_kernel(normed, zgate_w, gate_w, rate, silu, aux):
    inputs = normed[...]
    z = jnp.dot(inputs, zgate_w[...], preferred_element_type=f32)
    silu[...] = z * jax.nn.sigmoid(z)
    inputs = inputs.astype(f32)
    gates = gate_w[...].astype(f32)
    decay_in = jnp.sum(inputs * gates[0:1], axis=-1, keepdims=True)
    strength = jax.nn.sigmoid(jnp.sum(inputs * gates[1:2], axis=-1, keepdims=True))
    softplus = jnp.maximum(decay_in, 0.0) + jnp.log1p(jnp.exp(-jnp.abs(decay_in)))
    decay = -rate[0, 0] * softplus
    t = lax.broadcasted_iota(jnp.int32, (TOKS, LANES), 0)
    j = lax.broadcasted_iota(jnp.int32, (TOKS, LANES), 1)
    decay_row = jnp.sum(jnp.where(t == j, decay, 0.0), axis=0, keepdims=True)
    log_col = jnp.sum(jnp.where(j <= t, decay_row, 0.0), axis=1, keepdims=True)
    log_row = jnp.sum(jnp.where(t <= j, decay, 0.0), axis=0, keepdims=True)
    causal = j <= t
    ratio = jnp.where(causal, jnp.exp(jnp.where(causal, log_col - log_row, 0.0)), 0.0)
    last = jnp.sum(decay, axis=0, keepdims=True)
    ones = jnp.ones((TOKS, LANES), f32)
    aux[0] = jnp.where(j < t, strength * ratio, 0.0)
    aux[1] = ratio
    aux[2] = strength * ones
    aux[3] = jnp.exp(log_col) * ones
    aux[4] = jnp.exp(last - log_col) * ones
    aux[5] = jnp.exp(last) * ones


def solve_kernel(
    own, one, three, two, silu, aux, gain, out_w, part, sent, updates, key_scale_out,
    values, reads,
):
    columns = silu.shape[1]
    place = lax.axis_index(X)
    for piece, step in ((own, 0), (one, 1), (three, 3), (two, 2)):
        source = place ^ step
        held = piece[...].astype(f32)
        values[:, pl.ds(pl.multiple_of(source * columns, columns), columns)] = held[:TOKS, DK:]
        if step == 0:
            total, grams = held[:, :DK], held[TOKS:, DK:]
        else:
            coded = held[TOKS:, DK:]
            total = total + held[:, :DK]
            grams = grams + (coded + pltpu.roll(coded, grams.shape[1] - 64, 1))
    key_gram, cross_gram = grams[:, :LANES], grams[:, LANES:]
    t = lax.broadcasted_iota(jnp.int32, (TOKS, LANES), 0)
    j = lax.broadcasted_iota(jnp.int32, (TOKS, LANES), 1)
    diagonal = jnp.where(t == j, key_gram, 0.0)
    key_col = lax.rsqrt(jnp.sum(diagonal, axis=1, keepdims=True) + epsilon)
    key_row = lax.rsqrt(jnp.sum(diagonal, axis=0, keepdims=True) + epsilon)
    length = jnp.sum(jnp.where(j == TOKS, key_gram, 0.0), axis=1, keepdims=True)
    query_col = lax.rsqrt(length + epsilon) * DK ** (-0.5)
    key_scale_out[...] = key_col * jnp.ones((TOKS, LANES), f32)
    lower = aux[0] * key_gram * key_col * key_row
    mixing = aux[1] * cross_gram * query_col * key_row
    strength, grown, leftover = aux[2][:, :1], aux[3][:, :1], aux[4][:, :1]
    rest = strength * (values[...] - grown * (total[:TOKS] * key_col))
    readout = grown * (total[TOKS:] * query_col)
    solved = []
    for k in range(TOKS):
        update = rest[k : k + 1]
        solved.append(update)
        if k < TOKS - 1:
            rest = rest - lower[:, k : k + 1] * update
        readout = readout + mixing[:, k : k + 1] * update
    updates[...] = leftover * jnp.concatenate(solved, axis=0)
    reads[...] = readout
    inverse = lax.rsqrt(jnp.mean(readout * readout, axis=-1, keepdims=True) + epsilon)
    piece = reads[:, pl.ds(pl.multiple_of(place * columns, columns), columns)]
    gated = (piece * inverse * gain[...] * silu[...]).astype(bf16)
    partial = jnp.dot(gated, out_w[...], preferred_element_type=f32)
    part[...] = partial
    sent[...] = partial.astype(bf16)


def state_kernel(state, key, key_scale, updates, aux, out):
    normalized = key[...] * key_scale[:, :1]
    added = lax.dot_general(
        normalized, updates[...], (((0,), (0,)), ((), ())), precision=HIGHEST,
        preferred_element_type=f32,
    )
    out[...] = aux[5][:1, :1] * state[...] + added


def rows_sum_kernel(part, one, three, two, sent):
    result = (part[...] + two[...].astype(f32)) + (one[...].astype(f32) + three[...].astype(f32))
    sent[...] = result.astype(bf16)


def final_kernel(zero, one, three, two, hidden, gain, out):
    layer = (zero[...].astype(f32) + two[...].astype(f32)) + (
        one[...].astype(f32) + three[...].astype(f32)
    )
    stream = hidden[...].astype(f32) + layer
    inverse = lax.rsqrt(jnp.mean(stream * stream, axis=-1, keepdims=True) + epsilon)
    final = (stream * inverse * gain[...]).astype(bf16)
    for k in range(out.shape[0]):
        out[k] = final


def near_kernel(inputs, vocab_w, logits, lse):
    result = jnp.dot(inputs[...], vocab_w[...], preferred_element_type=f32)
    logits[...] = result
    peak = jnp.max(result, axis=-1, keepdims=True)
    total = peak + jnp.log(jnp.sum(jnp.exp(result - peak), axis=-1, keepdims=True))
    lse[...] = jnp.transpose(jnp.broadcast_to(total, (LANES, LANES)))[:8]


def far_kernel(inputs, vocab_w, near_lse, logits, lse):
    result = jnp.dot(inputs[...], vocab_w[...], preferred_element_type=f32)
    logits[...] = result
    peak = jnp.max(result, axis=-1, keepdims=True)
    total = peak + jnp.log(jnp.sum(jnp.exp(result - peak), axis=-1, keepdims=True))
    lse[0:1] = near_lse[0:1]
    lse[1:2] = jnp.transpose(jnp.broadcast_to(total, (LANES, LANES)))[0:1]


def chip_kernel(mine, other, out):
    a = mine[...]
    b = jnp.concatenate([other[1:2], other[0:1]], axis=0)
    peak = jnp.maximum(a, b)
    both = peak + jnp.log(jnp.exp(a - peak) + jnp.exp(b - peak))
    out[...] = jnp.broadcast_to(both[None], out.shape)


def score_kernel(everyone, near, far, out):
    core = lax.axis_index(C)
    parts = jnp.concatenate([everyone[:, 0, :], everyone[:, 1, :]], axis=1)
    peak = jnp.max(parts, axis=0, keepdims=True)
    total = peak + jnp.log(jnp.sum(jnp.exp(parts - peak), axis=0, keepdims=True))
    for k, logits in enumerate((near, far)):
        row = total[:, k * LANES : (k + 1) * LANES]
        column = jnp.transpose(jnp.broadcast_to(row, (LANES, LANES)))[:, :1]
        half = 1 - core if k == 0 else core
        for z in range(8):
            cut = slice(z * TOKS, (z + 1) * TOKS)
            out[2 * z + half] = logits[cut] - column[cut]


def on_device(
    hidden,
    norm_gain,
    query_weight,
    key_weight,
    value_weight,
    zgate_weight,
    gate_weight,
    decay_rate,
    output_gain,
    output_weight,
    recurrent_state,
    final_gain,
    vocab_weight,
):
    hidden = hidden[0]
    width = hidden.shape[1]
    columns = query_weight.shape[2]
    state = recurrent_state[0, 0, 0]
    vocab = vocab_weight.shape[1]
    other_hidden = swapped(hidden, C, 1)
    own, sent, normed, key = pl.pallas_call(
        project_kernel,
        out_shape=(
            shape((2 * TOKS, DK + columns)),
            shape((2 * TOKS, DK + columns), bf16),
            shape((TOKS, width), bf16),
            shape((TOKS, columns)),
        ),
        in_specs=[HB] * 6,
        out_specs=(VM, VM, VM, VM),
        scratch_shapes=[
            pltpu.VMEM((TOKS, width), bf16),
            pltpu.VMEM((1, width), f32),
            pltpu.VMEM((width, columns), bf16),
            pltpu.VMEM((width, columns), bf16),
            pltpu.VMEM((width, columns), bf16),
            pltpu.VMEM(state.shape, f32),
            pltpu.SemaphoreType.DMA((6,)),
        ],
        compiler_params=params(16),
        name="project",
    )(*in_hbm(hidden, norm_gain, key_weight[0], query_weight[0], value_weight[0], state))
    one, three, two = [swapped(sent, X, k) for k in (1, 3, 2)]
    silu, aux = pl.pallas_call(
        gate_kernel,
        out_shape=(shape((TOKS, columns)), shape((6, TOKS, LANES))),
        in_specs=[VM, VM, VM, SM],
        out_specs=(VM, VM),
        compiler_params=params(8),
        cost_estimate=cost(16 * 2048 * 512, 1 << 21),
        name="gates",
    )(normed, zgate_weight[0], gate_weight[0, :, :, 0], decay_rate)
    one, three, two, other_hidden = lax.optimization_barrier((one, three, two, other_hidden))
    part, sent, updates, key_scale = pl.pallas_call(
        solve_kernel,
        out_shape=(
            shape((TOKS, width)),
            shape((TOKS, width), bf16),
            shape((TOKS, DK)),
            shape((TOKS, LANES)),
        ),
        in_specs=[VM] * 8,
        out_specs=(VM,) * 4,
        scratch_shapes=[pltpu.VMEM((TOKS, DK), f32), pltpu.VMEM((TOKS, DK), f32)],
        compiler_params=params(8),
        name="solve",
    )(own, one, three, two, silu, aux, output_gain, output_weight[0])
    one, three, two = [swapped(sent, X, k) for k in (1, 3, 2)]
    new_state = pl.pallas_call(
        state_kernel,
        out_shape=shape(state.shape),
        in_specs=[VM] * 5,
        out_specs=VM,
        compiler_params=params(8),
        cost_estimate=cost(2 * 16 * 256 * 1024 * 6, 2 << 20),
        name="next_state",
    )(state, key, key_scale, updates, aux)
    one, three, two, new_state = lax.optimization_barrier((one, three, two, new_state))
    sent = pl.pallas_call(
        rows_sum_kernel,
        out_shape=shape((TOKS, width), bf16),
        in_specs=[VM] * 4,
        out_specs=VM,
        compiler_params=params(4),
        name="rows_sum",
    )(part, one, three, two)
    parts = [swapped(sent, (C, Y), 4 + k) for k in (0, 1, 3, 2)]
    final_in = pl.pallas_call(
        final_kernel,
        out_shape=shape((8, TOKS, width), bf16),
        in_specs=[VM] * 6,
        out_specs=VM,
        compiler_params=params(4),
        name="final_norm",
    )(*parts, other_hidden, final_gain[None])
    near = exchanged(final_in, Z).reshape(LANES, width)
    far = swapped(near, C, 1)
    near_logits, near_lse = pl.pallas_call(
        near_kernel,
        out_shape=(shape((LANES, vocab)), shape((8, LANES))),
        in_specs=[VM, VM],
        out_specs=(VM, VM),
        compiler_params=params(16),
        cost_estimate=cost(2 * 128 * 2048 * 512, 3 << 20),
        name="near_scores",
    )(near, vocab_weight)
    far_logits, lse = pl.pallas_call(
        far_kernel,
        out_shape=(shape((LANES, vocab)), shape((2, LANES))),
        in_specs=[VM, VM, VM],
        out_specs=(VM, VM),
        compiler_params=params(16),
        cost_estimate=cost(2 * 128 * 2048 * 512, 3 << 20),
        name="far_scores",
    )(far, vocab_weight, near_lse)
    other = swapped(lse, C, 1)
    chip = pl.pallas_call(
        chip_kernel,
        out_shape=shape((LANES, 2, LANES)),
        in_specs=[VM, VM],
        out_specs=VM,
        compiler_params=params(4),
        name="chip_total",
    )(lse, other)
    everyone = exchanged(chip, (Z, X, Y))
    log_probs = pl.pallas_call(
        score_kernel,
        out_shape=shape((16, TOKS, vocab)),
        in_specs=[VM] * 3,
        out_specs=VM,
        compiler_params=params(8),
        name="log_probs",
    )(everyone, near_logits, far_logits)
    return (new_state[None, None, None], log_probs)


def solution(mesh):
    split = Mesh(
        mesh.devices.reshape(8, 2, mesh.shape["rows"], mesh.shape["heads"]),
        ALL,
    )
    return jax.shard_map(
        on_device,
        mesh=split,
        in_specs=(
            P(DP, None, None),
            P(),
            P(None, None, (Y, X)),
            P(None, None, (Y, X)),
            P(None, None, (Y, X)),
            P(None, None, (Y, X)),
            P(None, None, None, Y),
            P(None, Y),
            P(None, X),
            P(None, (Y, X), None),
            P(None, DP, Y, X, None),
            P(),
            P(None, ALL),
        ),
        out_specs=(P(None, DP, Y, X, None), P(None, None, ALL)),
        check_vma=False,
    )
```

```python
import jax
import jax.numpy as jnp
from jax import lax
from jax.experimental import pallas as pl
from jax.experimental.pallas import tpu as pltpu
from jax.sharding import Mesh
from jax.sharding import PartitionSpec as P

Z, C, X, Y = ("dp_0", "dp_1", "rows", "heads")
DP = (Z, C)
ALL = (Z, C, X, Y)

TOKS = 16
DK = 1024
LANES = 128
epsilon = 1e-06
STEPS = (1, 3, 2)
f32, bf16 = jnp.float32, jnp.bfloat16
HIGHEST = lax.Precision.HIGHEST

VM = pl.BlockSpec(memory_space=pltpu.VMEM)
SM = pl.BlockSpec(memory_space=pltpu.SMEM)
HB = pl.BlockSpec(memory_space=pltpu.HBM)


def exchanged(parts, axes):
    return lax.all_to_all(parts, axes, 0, 0, tiled=True)


def swapped(shard, axis, step):
    return lax.ppermute(shard, axis, [(i, i ^ step) for i in range(lax.axis_size(axis))])


def in_hbm(*arrays):
    return [pltpu.with_memory_space_constraint(a, pltpu.HBM) for a in arrays]


def shape(dims, dtype=f32):
    return jax.ShapeDtypeStruct(dims, dtype)


def params(mib):
    return pltpu.CompilerParams(vmem_limit_bytes=mib << 20)


def cost(flops, size):
    return pl.CostEstimate(flops=flops, bytes_accessed=size, transcendentals=0)


def across(a, b):
    return lax.dot_general(
        a, b, (((1,), (1,)), ((), ())), precision=HIGHEST, preferred_element_type=f32
    )


def halves(a):
    high = a.astype(bf16)
    return high, (a - high.astype(f32)).astype(bf16)


def coded(a):
    high, low = halves(a)
    lane = lax.broadcasted_iota(jnp.int32, a.shape, 1) % LANES
    return jnp.where(lane < 64, high.astype(f32), pltpu.roll(low.astype(f32), 64, 1)).astype(bf16)


def decoded(a):
    a = a.astype(f32)
    return a + pltpu.roll(a, a.shape[1] - 64, 1)


def block_of(device, size):
    return pl.ds(pl.multiple_of(device * size, size), size)


def project_kernel(
    hidden, gain, key_w, query_w, value_w, state, own, sent_one, sent_three, sent_two,
    value_out, normed, key_out,
    hidden_v, gain_v, key_v, query_v, value_v, state_v, wide, sems,
):
    pairs = (
        (hidden, hidden_v), (gain, gain_v), (key_w, key_v), (query_w, query_v),
        (state, state_v), (value_w, value_v),
    )
    copies = [pltpu.make_async_copy(a, b, sems.at[i]) for i, (a, b) in enumerate(pairs)]
    for copy in copies:
        copy.start()
    copies[0].wait()
    copies[1].wait()
    x = hidden_v[...].astype(f32)
    inverse = lax.rsqrt(jnp.mean(x * x, axis=-1, keepdims=True) + epsilon)
    inputs = (x * inverse * gain_v[...]).astype(bf16)
    normed[...] = inputs
    copies[2].wait()
    key = jnp.dot(inputs, key_v[...], preferred_element_type=f32)
    key_out[...] = key
    copies[3].wait()
    query = jnp.dot(inputs, query_v[...], preferred_element_type=f32)
    both = jnp.concatenate([key, query], axis=0)
    wide_key = jnp.concatenate([key, jnp.zeros((LANES - TOKS, key.shape[1]), f32)], axis=0)
    grams = across(both, wide_key)
    length = jnp.sum(query * query, axis=-1, keepdims=True)
    lane = lax.broadcasted_iota(jnp.int32, (TOKS, LANES), 1)
    grams = jnp.concatenate(
        [jnp.where(lane == TOKS, length, grams[:TOKS]), grams[TOKS:]], axis=1
    )
    own[2 * TOKS :] = grams
    grams = coded(grams)
    high, low = halves(both)
    copies[4].wait()
    state_high, state_low = halves(state_v[...])
    first = jnp.dot(jnp.concatenate([high, low], axis=0), state_high, preferred_element_type=f32)
    second = jnp.dot(high, state_low, preferred_element_type=f32)
    wide[...] = first[: 2 * TOKS] + first[2 * TOKS :] + second
    place, columns = lax.axis_index(X), key.shape[1]
    own[: 2 * TOKS] = wide[:, block_of(place, columns)]
    for step, sent in zip(STEPS, (sent_one, sent_three, sent_two)):
        sent[: 2 * TOKS] = wide[:, block_of(place ^ step, columns)].astype(bf16)
        sent[2 * TOKS :] = grams
    copies[5].wait()
    value_out[...] = jnp.dot(inputs, value_v[...], preferred_element_type=f32)


def gate_kernel(normed, zgate_w, gate_w, rate, silu, aux):
    inputs = normed[...]
    z = jnp.dot(inputs, zgate_w[...], preferred_element_type=f32)
    silu[...] = z * jax.nn.sigmoid(z)
    inputs = inputs.astype(f32)
    gates = gate_w[...].astype(f32)
    decay_in = jnp.sum(inputs * gates[0:1], axis=-1, keepdims=True)
    strength = jax.nn.sigmoid(jnp.sum(inputs * gates[1:2], axis=-1, keepdims=True))
    softplus = jnp.maximum(decay_in, 0.0) + jnp.log1p(jnp.exp(-jnp.abs(decay_in)))
    decay = -rate[0, 0] * softplus
    t = lax.broadcasted_iota(jnp.int32, (TOKS, LANES), 0)
    j = lax.broadcasted_iota(jnp.int32, (TOKS, LANES), 1)
    decay_row = jnp.sum(jnp.where(t == j, decay, 0.0), axis=0, keepdims=True)
    log_col = jnp.sum(jnp.where(j <= t, decay_row, 0.0), axis=1, keepdims=True)
    log_row = jnp.sum(jnp.where(t <= j, decay, 0.0), axis=0, keepdims=True)
    causal = j <= t
    ratio = jnp.where(causal, jnp.exp(jnp.where(causal, log_col - log_row, 0.0)), 0.0)
    last = jnp.sum(decay, axis=0, keepdims=True)
    ones = jnp.ones((TOKS, LANES), f32)
    aux[0] = jnp.where(j < t, strength * ratio, 0.0)
    aux[1] = ratio
    aux[2] = strength * ones
    aux[3] = jnp.exp(log_col) * ones
    aux[4] = jnp.exp(last - log_col) * ones
    aux[5] = jnp.exp(last) * ones


def solve_kernel(
    own, one, three, two, value, silu, aux, gain, out_w, part, squares, update_out,
    key_scale_out, sent,
):
    total, grams = own[: 2 * TOKS], own[2 * TOKS :]
    for piece in (one, three, two):
        total = total + piece[: 2 * TOKS].astype(f32)
        grams = grams + decoded(piece[2 * TOKS :])
    key_gram, cross_gram = grams[:, :LANES], grams[:, LANES:]
    t = lax.broadcasted_iota(jnp.int32, (TOKS, LANES), 0)
    j = lax.broadcasted_iota(jnp.int32, (TOKS, LANES), 1)
    diagonal = jnp.where(t == j, key_gram, 0.0)
    key_col = lax.rsqrt(jnp.sum(diagonal, axis=1, keepdims=True) + epsilon)
    key_row = lax.rsqrt(jnp.sum(diagonal, axis=0, keepdims=True) + epsilon)
    length = jnp.sum(jnp.where(j == TOKS, key_gram, 0.0), axis=1, keepdims=True)
    query_col = lax.rsqrt(length + epsilon) * DK ** (-0.5)
    key_scale_out[...] = key_col * jnp.ones((TOKS, LANES), f32)
    lower = aux[0] * key_gram * key_col * key_row
    mixing = aux[1] * cross_gram * query_col * key_row
    strength, grown, leftover = aux[2][:, :1], aux[3][:, :1], aux[4][:, :1]
    rest = strength * (value[...] - grown * (total[:TOKS] * key_col))
    readout = grown * (total[TOKS:] * query_col)
    solved = []
    for k in range(TOKS):
        update = rest[k : k + 1]
        solved.append(update)
        if k < TOKS - 1:
            rest = rest - lower[:, k : k + 1] * update
        readout = readout + mixing[:, k : k + 1] * update
    gated = (readout * gain[...] * silu[...]).astype(bf16)
    partial = jnp.dot(gated, out_w[...], preferred_element_type=f32)
    width, columns = partial.shape[1], readout.shape[1]
    part[...] = partial
    sent[:, :width] = partial.astype(bf16)
    solved = leftover * jnp.concatenate(solved, axis=0)
    update_out[...] = solved
    sent[:, width : width + columns] = solved.astype(bf16)
    square = jnp.sum(readout * readout, axis=-1, keepdims=True) * jnp.ones((TOKS, LANES), f32)
    squares[...] = square
    sent[:, width + columns :] = coded(square)


def state_kernel(state, key, key_scale, updates, one, three, two, aux, out, wide):
    place = lax.axis_index(X)
    columns = updates.shape[1]
    start = one.shape[1] - LANES - columns
    wide[:, block_of(place, columns)] = updates[...]
    for step, piece in zip(STEPS, (one, three, two)):
        wide[:, block_of(place ^ step, columns)] = piece[:, start : start + columns].astype(f32)
    normalized = key[...] * key_scale[:, :1]
    added = lax.dot_general(
        normalized, wide[...], (((0,), (0,)), ((), ())), precision=HIGHEST,
        preferred_element_type=f32,
    )
    out[...] = aux[5][:1, :1] * state[...] + added


def rows_sum_kernel(part, squares, one, three, two, total, sent):
    width = part.shape[1]
    square, layer = squares[...], part[...]
    for piece in (one, three, two):
        layer = layer + piece[:, :width].astype(f32)
        square = square + decoded(piece[:, piece.shape[1] - LANES :])
    result = layer * lax.rsqrt(square[:, :1] / DK + epsilon)
    total[...] = result
    sent[...] = result.astype(bf16)


def final_kernel(total, one, three, two, hidden, gain, out):
    layer = (total[...] + two[...].astype(f32)) + (one[...].astype(f32) + three[...].astype(f32))
    stream = hidden[...].astype(f32) + layer
    inverse = lax.rsqrt(jnp.mean(stream * stream, axis=-1, keepdims=True) + epsilon)
    final = (stream * inverse * gain[...]).astype(bf16)
    for k in range(out.shape[0]):
        out[k] = final


def near_kernel(inputs, vocab_w, logits, lse):
    result = jnp.dot(inputs[...], vocab_w[...], preferred_element_type=f32)
    logits[...] = result
    peak = jnp.max(result, axis=-1, keepdims=True)
    total = peak + jnp.log(jnp.sum(jnp.exp(result - peak), axis=-1, keepdims=True))
    lse[...] = jnp.transpose(jnp.broadcast_to(total, (LANES, LANES)))[:8]


def far_kernel(inputs, vocab_w, near_lse, logits, lse):
    result = jnp.dot(inputs[...], vocab_w[...], preferred_element_type=f32)
    logits[...] = result
    peak = jnp.max(result, axis=-1, keepdims=True)
    total = peak + jnp.log(jnp.sum(jnp.exp(result - peak), axis=-1, keepdims=True))
    lse[0:1] = near_lse[0:1]
    lse[1:2] = jnp.transpose(jnp.broadcast_to(total, (LANES, LANES)))[0:1]


def chip_kernel(mine, other, out):
    a = mine[...]
    b = jnp.concatenate([other[1:2], other[0:1]], axis=0)
    peak = jnp.maximum(a, b)
    both = peak + jnp.log(jnp.exp(a - peak) + jnp.exp(b - peak))
    out[...] = jnp.broadcast_to(both[None], out.shape)


def score_kernel(everyone, near, far, out):
    core = lax.axis_index(C)
    parts = jnp.concatenate([everyone[:, 0, :], everyone[:, 1, :]], axis=1)
    peak = jnp.max(parts, axis=0, keepdims=True)
    total = peak + jnp.log(jnp.sum(jnp.exp(parts - peak), axis=0, keepdims=True))
    for k, logits in enumerate((near, far)):
        row = total[:, k * LANES : (k + 1) * LANES]
        column = jnp.transpose(jnp.broadcast_to(row, (LANES, LANES)))[:, :1]
        half = core if k == 0 else 1 - core
        for z in range(8):
            cut = slice(z * TOKS, (z + 1) * TOKS)
            out[2 * z + half] = logits[cut] - column[cut]


def on_device(
    hidden,
    norm_gain,
    query_weight,
    key_weight,
    value_weight,
    zgate_weight,
    gate_weight,
    decay_rate,
    output_gain,
    output_weight,
    recurrent_state,
    final_gain,
    vocab_weight,
):
    hidden = hidden[0]
    width = hidden.shape[1]
    columns = query_weight.shape[2]
    state = recurrent_state[0, 0, 0]
    vocab = vocab_weight.shape[1]
    packet = shape((3 * TOKS, columns), bf16)
    own, *sent, value, normed, key = pl.pallas_call(
        project_kernel,
        out_shape=(
            shape((3 * TOKS, columns)),
            packet,
            packet,
            packet,
            shape((TOKS, columns)),
            shape((TOKS, width), bf16),
            shape((TOKS, columns)),
        ),
        in_specs=[HB] * 6,
        out_specs=(VM,) * 7,
        scratch_shapes=[
            pltpu.VMEM((TOKS, width), bf16),
            pltpu.VMEM((1, width), f32),
            pltpu.VMEM((width, columns), bf16),
            pltpu.VMEM((width, columns), bf16),
            pltpu.VMEM((width, columns), bf16),
            pltpu.VMEM(state.shape, f32),
            pltpu.VMEM((2 * TOKS, DK), f32),
            pltpu.SemaphoreType.DMA((6,)),
        ],
        compiler_params=params(16),
        name="project",
    )(*in_hbm(hidden, norm_gain, key_weight[0], query_weight[0], value_weight[0], state))
    one, three, two = [swapped(a, X, k) for a, k in zip(sent, STEPS)]
    silu, aux = pl.pallas_call(
        gate_kernel,
        out_shape=(shape((TOKS, columns)), shape((6, TOKS, LANES))),
        in_specs=[VM, VM, VM, SM],
        out_specs=(VM, VM),
        compiler_params=params(8),
        cost_estimate=cost(16 * 2048 * 512, 1 << 21),
        name="gates",
    )(normed, zgate_weight[0], gate_weight[0, :, :, 0], decay_rate)
    part, squares, updates, key_scale, sent = pl.pallas_call(
        solve_kernel,
        out_shape=(
            shape((TOKS, width)),
            shape((TOKS, LANES)),
            shape((TOKS, columns)),
            shape((TOKS, LANES)),
            shape((TOKS, width + columns + LANES), bf16),
        ),
        in_specs=[VM] * 9,
        out_specs=(VM,) * 5,
        compiler_params=params(8),
        name="solve",
    )(own, one, three, two, value, silu, aux, output_gain, output_weight[0])
    one, three, two = [swapped(sent, X, k) for k in STEPS]
    total, sent = pl.pallas_call(
        rows_sum_kernel,
        out_shape=(shape((TOKS, width)), shape((TOKS, width), bf16)),
        in_specs=[VM] * 5,
        out_specs=(VM, VM),
        compiler_params=params(4),
        name="rows_sum",
    )(part, squares, one, three, two)
    new_state = pl.pallas_call(
        state_kernel,
        out_shape=shape(state.shape),
        in_specs=[VM] * 8,
        out_specs=VM,
        scratch_shapes=[pltpu.VMEM((TOKS, DK), f32)],
        compiler_params=params(8),
        cost_estimate=cost(2 * 16 * 256 * 1024 * 6, 2 << 20),
        name="next_state",
    )(state, key, key_scale, updates, one, three, two, aux)
    one, three, two = [swapped(sent, Y, k) for k in STEPS]
    one, three, two, new_state = lax.optimization_barrier((one, three, two, new_state))
    final_in = pl.pallas_call(
        final_kernel,
        out_shape=shape((8, TOKS, width), bf16),
        in_specs=[VM] * 6,
        out_specs=VM,
        compiler_params=params(4),
        name="final_norm",
    )(total, one, three, two, hidden, final_gain[None])
    near = exchanged(final_in, Z).reshape(LANES, width)
    far = swapped(near, C, 1)
    near_logits, near_lse = pl.pallas_call(
        near_kernel,
        out_shape=(shape((LANES, vocab)), shape((8, LANES))),
        in_specs=[VM, VM],
        out_specs=(VM, VM),
        compiler_params=params(16),
        cost_estimate=cost(2 * 128 * 2048 * 512, 3 << 20),
        name="near_scores",
    )(near, vocab_weight)
    far_logits, lse = pl.pallas_call(
        far_kernel,
        out_shape=(shape((LANES, vocab)), shape((2, LANES))),
        in_specs=[VM, VM, VM],
        out_specs=(VM, VM),
        compiler_params=params(16),
        cost_estimate=cost(2 * 128 * 2048 * 512, 3 << 20),
        name="far_scores",
    )(far, vocab_weight, near_lse)
    other = swapped(lse, C, 1)
    chip = pl.pallas_call(
        chip_kernel,
        out_shape=shape((LANES, 2, LANES)),
        in_specs=[VM, VM],
        out_specs=VM,
        compiler_params=params(4),
        name="chip_total",
    )(lse, other)
    everyone = exchanged(chip, (Z, X, Y))
    log_probs = pl.pallas_call(
        score_kernel,
        out_shape=shape((16, TOKS, vocab)),
        in_specs=[VM] * 3,
        out_specs=VM,
        compiler_params=params(8),
        name="log_probs",
    )(everyone, near_logits, far_logits)
    return (new_state[None, None, None], log_probs)


def solution(mesh):
    split = Mesh(
        mesh.devices.reshape(8, 2, mesh.shape["rows"], mesh.shape["heads"]),
        ALL,
    )
    return jax.shard_map(
        on_device,
        mesh=split,
        in_specs=(
            P(DP, None, None),
            P(),
            P(None, None, (Y, X)),
            P(None, None, (Y, X)),
            P(None, None, (Y, X)),
            P(None, None, (Y, X)),
            P(None, None, None, Y),
            P(None, Y),
            P(None, X),
            P(None, (Y, X), None),
            P(None, DP, Y, X, None),
            P(),
            P(None, ALL),
        ),
        out_specs=(P(None, DP, Y, X, None), P(None, None, ALL)),
        check_vma=False,
    )
```

```python
import jax
import jax.numpy as jnp
from jax import lax
from jax.experimental import pallas as pl
from jax.experimental.pallas import tpu as pltpu
from jax.sharding import Mesh
from jax.sharding import PartitionSpec as P

Z, C, X, Y = ("dp_0", "dp_1", "rows", "heads")
DP = (Z, C)
ALL = (Z, C, X, Y)

TOKS = 16
DK = 1024
LANES = 128
epsilon = 1e-06
STEPS = (1, 3, 2)
f32, bf16 = jnp.float32, jnp.bfloat16
HIGHEST = lax.Precision.HIGHEST

VM = pl.BlockSpec(memory_space=pltpu.VMEM)
SM = pl.BlockSpec(memory_space=pltpu.SMEM)
HB = pl.BlockSpec(memory_space=pltpu.HBM)


def exchanged(parts, axes):
    return lax.all_to_all(parts, axes, 0, 0, tiled=True)


def swapped(shard, axis, step):
    return lax.ppermute(shard, axis, [(i, i ^ step) for i in range(lax.axis_size(axis))])


def in_hbm(*arrays):
    return [pltpu.with_memory_space_constraint(a, pltpu.HBM) for a in arrays]


def shape(dims, dtype=f32):
    return jax.ShapeDtypeStruct(dims, dtype)


def params(mib):
    return pltpu.CompilerParams(vmem_limit_bytes=mib << 20)


def cost(flops, size):
    return pl.CostEstimate(flops=flops, bytes_accessed=size, transcendentals=0)


def across(a, b):
    return lax.dot_general(
        a, b, (((1,), (1,)), ((), ())), precision=HIGHEST, preferred_element_type=f32
    )


def halves(a):
    high = a.astype(bf16)
    return high, (a - high.astype(f32)).astype(bf16)


def coded(a):
    high, low = halves(a)
    lane = lax.broadcasted_iota(jnp.int32, a.shape, 1) % LANES
    return jnp.where(lane < 64, high.astype(f32), pltpu.roll(low.astype(f32), 64, 1)).astype(bf16)


def decoded(a):
    a = a.astype(f32)
    return a + pltpu.roll(a, a.shape[1] - 64, 1)


def block_of(device, size):
    return pl.ds(pl.multiple_of(device * size, size), size)


def project_kernel(
    hidden, gain, key_w, query_w, state, own, sent_one, sent_three, sent_two, normed, key_out,
    hidden_v, gain_v, key_v, query_v, state_v, wide, sems,
):
    pairs = (
        (hidden, hidden_v), (gain, gain_v), (key_w, key_v), (query_w, query_v),
        (state, state_v),
    )
    copies = [pltpu.make_async_copy(a, b, sems.at[i]) for i, (a, b) in enumerate(pairs)]
    for copy in copies:
        copy.start()
    copies[0].wait()
    copies[1].wait()
    x = hidden_v[...].astype(f32)
    inverse = lax.rsqrt(jnp.mean(x * x, axis=-1, keepdims=True) + epsilon)
    inputs = (x * inverse * gain_v[...]).astype(bf16)
    normed[...] = inputs
    copies[2].wait()
    key = jnp.dot(inputs, key_v[...], preferred_element_type=f32)
    key_out[...] = key
    copies[3].wait()
    query = jnp.dot(inputs, query_v[...], preferred_element_type=f32)
    both = jnp.concatenate([key, query], axis=0)
    wide_key = jnp.concatenate([key, jnp.zeros((LANES - TOKS, key.shape[1]), f32)], axis=0)
    grams = across(both, wide_key)
    length = jnp.sum(query * query, axis=-1, keepdims=True)
    lane = lax.broadcasted_iota(jnp.int32, (TOKS, LANES), 1)
    grams = jnp.concatenate(
        [jnp.where(lane == TOKS, length, grams[:TOKS]), grams[TOKS:]], axis=1
    )
    own[2 * TOKS :] = grams
    grams = coded(grams)
    high, low = halves(both)
    copies[4].wait()
    state_high, state_low = halves(state_v[...])
    first = jnp.dot(jnp.concatenate([high, low], axis=0), state_high, preferred_element_type=f32)
    second = jnp.dot(high, state_low, preferred_element_type=f32)
    wide[...] = first[: 2 * TOKS] + first[2 * TOKS :] + second
    place, columns = lax.axis_index(X), key.shape[1]
    own[: 2 * TOKS] = wide[:, block_of(place, columns)]
    for step, sent in zip(STEPS, (sent_one, sent_three, sent_two)):
        sent[: 2 * TOKS] = wide[:, block_of(place ^ step, columns)].astype(bf16)
        sent[2 * TOKS :] = grams


def gate_kernel(
    normed, zgate_w, value_w, gate_w, rate, silu, value, aux, zgate_v, value_v, sems,
):
    copies = [
        pltpu.make_async_copy(zgate_w, zgate_v, sems.at[0]),
        pltpu.make_async_copy(value_w, value_v, sems.at[1]),
    ]
    for copy in copies:
        copy.start()
    inputs = normed[...]
    inputs = inputs.astype(f32)
    gates = gate_w[...].astype(f32)
    decay_in = jnp.sum(inputs * gates[0:1], axis=-1, keepdims=True)
    strength = jax.nn.sigmoid(jnp.sum(inputs * gates[1:2], axis=-1, keepdims=True))
    softplus = jnp.maximum(decay_in, 0.0) + jnp.log1p(jnp.exp(-jnp.abs(decay_in)))
    decay = -rate[0, 0] * softplus
    t = lax.broadcasted_iota(jnp.int32, (TOKS, LANES), 0)
    j = lax.broadcasted_iota(jnp.int32, (TOKS, LANES), 1)
    decay_row = jnp.sum(jnp.where(t == j, decay, 0.0), axis=0, keepdims=True)
    log_col = jnp.sum(jnp.where(j <= t, decay_row, 0.0), axis=1, keepdims=True)
    log_row = jnp.sum(jnp.where(t <= j, decay, 0.0), axis=0, keepdims=True)
    causal = j <= t
    ratio = jnp.where(causal, jnp.exp(jnp.where(causal, log_col - log_row, 0.0)), 0.0)
    last = jnp.sum(decay, axis=0, keepdims=True)
    ones = jnp.ones((TOKS, LANES), f32)
    aux[0] = jnp.where(j < t, strength * ratio, 0.0)
    aux[1] = ratio
    aux[2] = strength * ones
    aux[3] = jnp.exp(log_col) * ones
    aux[4] = jnp.exp(last - log_col) * ones
    aux[5] = jnp.exp(last) * ones
    copies[0].wait()
    z = jnp.dot(normed[...], zgate_v[...], preferred_element_type=f32)
    silu[...] = z * jax.nn.sigmoid(z)
    copies[1].wait()
    value[...] = jnp.dot(normed[...], value_v[...], preferred_element_type=f32)


def solve_kernel(
    own, one, three, two, value, silu, aux, gain, out_w, part, squares, update_out,
    key_scale_out, sent,
):
    total, grams = own[: 2 * TOKS], own[2 * TOKS :]
    for piece in (one, three, two):
        total = total + piece[: 2 * TOKS].astype(f32)
        grams = grams + decoded(piece[2 * TOKS :])
    key_gram, cross_gram = grams[:, :LANES], grams[:, LANES:]
    t = lax.broadcasted_iota(jnp.int32, (TOKS, LANES), 0)
    j = lax.broadcasted_iota(jnp.int32, (TOKS, LANES), 1)
    diagonal = jnp.where(t == j, key_gram, 0.0)
    key_col = lax.rsqrt(jnp.sum(diagonal, axis=1, keepdims=True) + epsilon)
    key_row = lax.rsqrt(jnp.sum(diagonal, axis=0, keepdims=True) + epsilon)
    length = jnp.sum(jnp.where(j == TOKS, key_gram, 0.0), axis=1, keepdims=True)
    query_col = lax.rsqrt(length + epsilon) * DK ** (-0.5)
    key_scale_out[...] = key_col * jnp.ones((TOKS, LANES), f32)
    lower = aux[0] * key_gram * key_col * key_row
    mixing = aux[1] * cross_gram * query_col * key_row
    strength, grown, leftover = aux[2][:, :1], aux[3][:, :1], aux[4][:, :1]
    rest = strength * (value[...] - grown * (total[:TOKS] * key_col))
    readout = grown * (total[TOKS:] * query_col)
    solved = []
    for k in range(TOKS):
        update = rest[k : k + 1]
        solved.append(update)
        if k < TOKS - 1:
            rest = rest - lower[:, k : k + 1] * update
        readout = readout + mixing[:, k : k + 1] * update
    gated = (readout * gain[...] * silu[...]).astype(bf16)
    partial = jnp.dot(gated, out_w[...], preferred_element_type=f32)
    width, columns = partial.shape[1], readout.shape[1]
    part[...] = partial
    sent[:, :width] = partial.astype(bf16)
    solved = leftover * jnp.concatenate(solved, axis=0)
    update_out[...] = solved
    sent[:, width : width + columns] = solved.astype(bf16)
    square = jnp.sum(readout * readout, axis=-1, keepdims=True) * jnp.ones((TOKS, LANES), f32)
    squares[...] = square
    sent[:, width + columns :] = coded(square)


def state_kernel(state, key, key_scale, updates, one, three, two, aux, out, wide):
    place = lax.axis_index(X)
    columns = updates.shape[1]
    start = one.shape[1] - LANES - columns
    wide[:, block_of(place, columns)] = updates[...]
    for step, piece in zip(STEPS, (one, three, two)):
        wide[:, block_of(place ^ step, columns)] = piece[:, start : start + columns].astype(f32)
    normalized = key[...] * key_scale[:, :1]
    added = lax.dot_general(
        normalized, wide[...], (((0,), (0,)), ((), ())), precision=HIGHEST,
        preferred_element_type=f32,
    )
    out[...] = aux[5][:1, :1] * state[...] + added


def rows_sum_kernel(part, squares, one, three, two, total, sent):
    width = part.shape[1]
    square, layer = squares[...], part[...]
    for piece in (one, three, two):
        layer = layer + piece[:, :width].astype(f32)
        square = square + decoded(piece[:, piece.shape[1] - LANES :])
    result = layer * lax.rsqrt(square[:, :1] / DK + epsilon)
    total[...] = result
    sent[...] = result.astype(bf16)


def final_kernel(total, one, three, two, hidden, gain, out):
    layer = (total[...] + two[...].astype(f32)) + (one[...].astype(f32) + three[...].astype(f32))
    stream = hidden[...].astype(f32) + layer
    inverse = lax.rsqrt(jnp.mean(stream * stream, axis=-1, keepdims=True) + epsilon)
    final = (stream * inverse * gain[...]).astype(bf16)
    for k in range(out.shape[0]):
        out[k] = final


def near_kernel(inputs, vocab_w, logits, lse):
    result = jnp.dot(inputs[...], vocab_w[...], preferred_element_type=f32)
    logits[...] = result
    peak = jnp.max(result, axis=-1, keepdims=True)
    total = peak + jnp.log(jnp.sum(jnp.exp(result - peak), axis=-1, keepdims=True))
    lse[...] = jnp.transpose(jnp.broadcast_to(total, (LANES, LANES)))[:8]


def far_kernel(inputs, vocab_w, near_lse, logits, lse):
    result = jnp.dot(inputs[...], vocab_w[...], preferred_element_type=f32)
    logits[...] = result
    peak = jnp.max(result, axis=-1, keepdims=True)
    total = peak + jnp.log(jnp.sum(jnp.exp(result - peak), axis=-1, keepdims=True))
    lse[0:1] = near_lse[0:1]
    lse[1:2] = jnp.transpose(jnp.broadcast_to(total, (LANES, LANES)))[0:1]


def chip_kernel(mine, other, out):
    a = mine[...]
    b = jnp.concatenate([other[1:2], other[0:1]], axis=0)
    peak = jnp.maximum(a, b)
    both = peak + jnp.log(jnp.exp(a - peak) + jnp.exp(b - peak))
    out[...] = jnp.broadcast_to(both[None], out.shape)


def score_kernel(everyone, near, far, out):
    core = lax.axis_index(C)
    parts = jnp.concatenate([everyone[:, 0, :], everyone[:, 1, :]], axis=1)
    peak = jnp.max(parts, axis=0, keepdims=True)
    total = peak + jnp.log(jnp.sum(jnp.exp(parts - peak), axis=0, keepdims=True))
    for k, logits in enumerate((near, far)):
        row = total[:, k * LANES : (k + 1) * LANES]
        column = jnp.transpose(jnp.broadcast_to(row, (LANES, LANES)))[:, :1]
        half = core if k == 0 else 1 - core
        for z in range(8):
            cut = slice(z * TOKS, (z + 1) * TOKS)
            out[2 * z + half] = logits[cut] - column[cut]


def on_device(
    hidden,
    norm_gain,
    query_weight,
    key_weight,
    value_weight,
    zgate_weight,
    gate_weight,
    decay_rate,
    output_gain,
    output_weight,
    recurrent_state,
    final_gain,
    vocab_weight,
):
    hidden = hidden[0]
    width = hidden.shape[1]
    columns = query_weight.shape[2]
    state = recurrent_state[0, 0, 0]
    vocab = vocab_weight.shape[1]
    packet = shape((3 * TOKS, columns), bf16)
    own, *sent, normed, key = pl.pallas_call(
        project_kernel,
        out_shape=(
            shape((3 * TOKS, columns)),
            packet,
            packet,
            packet,
            shape((TOKS, width), bf16),
            shape((TOKS, columns)),
        ),
        in_specs=[HB] * 5,
        out_specs=(VM,) * 6,
        scratch_shapes=[
            pltpu.VMEM((TOKS, width), bf16),
            pltpu.VMEM((1, width), f32),
            pltpu.VMEM((width, columns), bf16),
            pltpu.VMEM((width, columns), bf16),
            pltpu.VMEM(state.shape, f32),
            pltpu.VMEM((2 * TOKS, DK), f32),
            pltpu.SemaphoreType.DMA((5,)),
        ],
        compiler_params=params(16),
        name="project",
    )(*in_hbm(hidden, norm_gain, key_weight[0], query_weight[0], state))
    one, three, two = [swapped(a, X, k) for a, k in zip(sent, STEPS)]
    silu, value, aux = pl.pallas_call(
        gate_kernel,
        out_shape=(shape((TOKS, columns)), shape((TOKS, columns)), shape((6, TOKS, LANES))),
        in_specs=[VM, HB, HB, VM, SM],
        out_specs=(VM, VM, VM),
        scratch_shapes=[
            pltpu.VMEM((width, columns), bf16),
            pltpu.VMEM((width, columns), bf16),
            pltpu.SemaphoreType.DMA((2,)),
        ],
        compiler_params=params(8),
        cost_estimate=cost(16 * 2048 * 1024, 2 << 20),
        name="gates",
    )(normed, *in_hbm(zgate_weight[0], value_weight[0]), gate_weight[0, :, :, 0], decay_rate)
    part, squares, updates, key_scale, sent = pl.pallas_call(
        solve_kernel,
        out_shape=(
            shape((TOKS, width)),
            shape((TOKS, LANES)),
            shape((TOKS, columns)),
            shape((TOKS, LANES)),
            shape((TOKS, width + columns + LANES), bf16),
        ),
        in_specs=[VM] * 9,
        out_specs=(VM,) * 5,
        compiler_params=params(8),
        name="solve",
    )(own, one, three, two, value, silu, aux, output_gain, output_weight[0])
    one, three, two = [swapped(sent, X, k) for k in STEPS]
    total, sent = pl.pallas_call(
        rows_sum_kernel,
        out_shape=(shape((TOKS, width)), shape((TOKS, width), bf16)),
        in_specs=[VM] * 5,
        out_specs=(VM, VM),
        compiler_params=params(4),
        name="rows_sum",
    )(part, squares, one, three, two)
    new_state = pl.pallas_call(
        state_kernel,
        out_shape=shape(state.shape),
        in_specs=[VM] * 8,
        out_specs=VM,
        scratch_shapes=[pltpu.VMEM((TOKS, DK), f32)],
        compiler_params=params(8),
        cost_estimate=cost(2 * 16 * 256 * 1024 * 6, 2 << 20),
        name="next_state",
    )(state, key, key_scale, updates, one, three, two, aux)
    one, three, two = [swapped(sent, Y, k) for k in STEPS]
    one, three, two, new_state = lax.optimization_barrier((one, three, two, new_state))
    final_in = pl.pallas_call(
        final_kernel,
        out_shape=shape((8, TOKS, width), bf16),
        in_specs=[VM] * 6,
        out_specs=VM,
        compiler_params=params(4),
        name="final_norm",
    )(total, one, three, two, hidden, final_gain[None])
    near = exchanged(final_in, Z).reshape(LANES, width)
    far = swapped(near, C, 1)
    near_logits, near_lse = pl.pallas_call(
        near_kernel,
        out_shape=(shape((LANES, vocab)), shape((8, LANES))),
        in_specs=[VM, VM],
        out_specs=(VM, VM),
        compiler_params=params(16),
        cost_estimate=cost(2 * 128 * 2048 * 512, 3 << 20),
        name="near_scores",
    )(near, vocab_weight)
    far_logits, lse = pl.pallas_call(
        far_kernel,
        out_shape=(shape((LANES, vocab)), shape((2, LANES))),
        in_specs=[VM, VM, VM],
        out_specs=(VM, VM),
        compiler_params=params(16),
        cost_estimate=cost(2 * 128 * 2048 * 512, 3 << 20),
        name="far_scores",
    )(far, vocab_weight, near_lse)
    other = swapped(lse, C, 1)
    chip = pl.pallas_call(
        chip_kernel,
        out_shape=shape((LANES, 2, LANES)),
        in_specs=[VM, VM],
        out_specs=VM,
        compiler_params=params(4),
        name="chip_total",
    )(lse, other)
    everyone = exchanged(chip, (Z, X, Y))
    log_probs = pl.pallas_call(
        score_kernel,
        out_shape=shape((16, TOKS, vocab)),
        in_specs=[VM] * 3,
        out_specs=VM,
        compiler_params=params(8),
        name="log_probs",
    )(everyone, near_logits, far_logits)
    return (new_state[None, None, None], log_probs)


def solution(mesh):
    split = Mesh(
        mesh.devices.reshape(8, 2, mesh.shape["rows"], mesh.shape["heads"]),
        ALL,
    )
    return jax.shard_map(
        on_device,
        mesh=split,
        in_specs=(
            P(DP, None, None),
            P(),
            P(None, None, (Y, X)),
            P(None, None, (Y, X)),
            P(None, None, (Y, X)),
            P(None, None, (Y, X)),
            P(None, None, None, Y),
            P(None, Y),
            P(None, X),
            P(None, (Y, X), None),
            P(None, DP, Y, X, None),
            P(),
            P(None, ALL),
        ),
        out_specs=(P(None, DP, Y, X, None), P(None, None, ALL)),
        check_vma=False,
    )
```

```python
import jax
import jax.numpy as jnp
from jax import lax
from jax.experimental import pallas as pl
from jax.experimental.pallas import tpu as pltpu
from jax.sharding import Mesh
from jax.sharding import PartitionSpec as P

Z, C, X, Y = ("dp_0", "dp_1", "rows", "heads")
DP = (Z, C)
ALL = (Z, C, X, Y)

TOKS = 16
DK = 1024
LANES = 128
epsilon = 1e-06
STEPS = (1, 3, 2)
Z_STEPS = (1, 3, 2, 6, 7, 5, 4)
f32, bf16 = jnp.float32, jnp.bfloat16
HIGHEST = lax.Precision.HIGHEST

VM = pl.BlockSpec(memory_space=pltpu.VMEM)
SM = pl.BlockSpec(memory_space=pltpu.SMEM)
HB = pl.BlockSpec(memory_space=pltpu.HBM)


def exchanged(parts, axes):
    return lax.all_to_all(parts, axes, 0, 0, tiled=True)


def swapped(shard, axis, step):
    return lax.ppermute(shard, axis, [(i, i ^ step) for i in range(lax.axis_size(axis))])


def in_hbm(*arrays):
    return [pltpu.with_memory_space_constraint(a, pltpu.HBM) for a in arrays]


def shape(dims, dtype=f32):
    return jax.ShapeDtypeStruct(dims, dtype)


def params(mib):
    return pltpu.CompilerParams(vmem_limit_bytes=mib << 20)


def cost(flops, size):
    return pl.CostEstimate(flops=flops, bytes_accessed=size, transcendentals=0)


def across(a, b):
    return lax.dot_general(
        a, b, (((1,), (1,)), ((), ())), precision=HIGHEST, preferred_element_type=f32
    )


def halves(a):
    high = a.astype(bf16)
    return high, (a - high.astype(f32)).astype(bf16)


def coded(a):
    high, low = halves(a)
    lane = lax.broadcasted_iota(jnp.int32, a.shape, 1) % LANES
    return jnp.where(lane < 64, high.astype(f32), pltpu.roll(low.astype(f32), 64, 1)).astype(bf16)


def decoded(a):
    a = a.astype(f32)
    return a + pltpu.roll(a, a.shape[1] - 64, 1)


def block_of(device, size):
    return pl.ds(pl.multiple_of(device * size, size), size)


def project_kernel(
    hidden, gain, key_w, query_w, state, own, sent_one, sent_three, sent_two, normed, key_out,
    hidden_v, gain_v, key_v, query_v, state_v, wide, sems,
):
    pairs = (
        (hidden, hidden_v), (gain, gain_v), (key_w, key_v), (query_w, query_v),
        (state, state_v),
    )
    copies = [pltpu.make_async_copy(a, b, sems.at[i]) for i, (a, b) in enumerate(pairs)]
    for copy in copies:
        copy.start()
    copies[0].wait()
    copies[1].wait()
    x = hidden_v[...].astype(f32)
    inverse = lax.rsqrt(jnp.mean(x * x, axis=-1, keepdims=True) + epsilon)
    inputs = (x * inverse * gain_v[...]).astype(bf16)
    normed[...] = inputs
    copies[2].wait()
    key = jnp.dot(inputs, key_v[...], preferred_element_type=f32)
    key_out[...] = key
    copies[3].wait()
    query = jnp.dot(inputs, query_v[...], preferred_element_type=f32)
    both = jnp.concatenate([key, query], axis=0)
    wide_key = jnp.concatenate([key, jnp.zeros((LANES - TOKS, key.shape[1]), f32)], axis=0)
    grams = across(both, wide_key)
    length = jnp.sum(query * query, axis=-1, keepdims=True)
    lane = lax.broadcasted_iota(jnp.int32, (TOKS, LANES), 1)
    grams = jnp.concatenate(
        [jnp.where(lane == TOKS, length, grams[:TOKS]), grams[TOKS:]], axis=1
    )
    own[2 * TOKS :] = grams
    grams = coded(grams)
    high, low = halves(both)
    copies[4].wait()
    state_high, state_low = halves(state_v[...])
    first = jnp.dot(jnp.concatenate([high, low], axis=0), state_high, preferred_element_type=f32)
    second = jnp.dot(high, state_low, preferred_element_type=f32)
    wide[...] = first[: 2 * TOKS] + first[2 * TOKS :] + second
    place, columns = lax.axis_index(X), key.shape[1]
    own[: 2 * TOKS] = wide[:, block_of(place, columns)]
    for step, sent in zip(STEPS, (sent_one, sent_three, sent_two)):
        sent[: 2 * TOKS] = wide[:, block_of(place ^ step, columns)].astype(bf16)
        sent[2 * TOKS :] = grams


def gate_kernel(
    normed, zgate_w, value_w, gate_w, rate, silu, value, aux, zgate_v, value_v, sems,
):
    copies = [
        pltpu.make_async_copy(zgate_w, zgate_v, sems.at[0]),
        pltpu.make_async_copy(value_w, value_v, sems.at[1]),
    ]
    for copy in copies:
        copy.start()
    inputs = normed[...]
    inputs = inputs.astype(f32)
    gates = gate_w[...].astype(f32)
    decay_in = jnp.sum(inputs * gates[0:1], axis=-1, keepdims=True)
    strength = jax.nn.sigmoid(jnp.sum(inputs * gates[1:2], axis=-1, keepdims=True))
    softplus = jnp.maximum(decay_in, 0.0) + jnp.log1p(jnp.exp(-jnp.abs(decay_in)))
    decay = -rate[0, 0] * softplus
    t = lax.broadcasted_iota(jnp.int32, (TOKS, LANES), 0)
    j = lax.broadcasted_iota(jnp.int32, (TOKS, LANES), 1)
    decay_row = jnp.sum(jnp.where(t == j, decay, 0.0), axis=0, keepdims=True)
    log_col = jnp.sum(jnp.where(j <= t, decay_row, 0.0), axis=1, keepdims=True)
    log_row = jnp.sum(jnp.where(t <= j, decay, 0.0), axis=0, keepdims=True)
    causal = j <= t
    ratio = jnp.where(causal, jnp.exp(jnp.where(causal, log_col - log_row, 0.0)), 0.0)
    last = jnp.sum(decay, axis=0, keepdims=True)
    ones = jnp.ones((TOKS, LANES), f32)
    aux[0] = jnp.where(j < t, strength * ratio, 0.0)
    aux[1] = ratio
    aux[2] = strength * ones
    aux[3] = jnp.exp(log_col) * ones
    aux[4] = jnp.exp(last - log_col) * ones
    aux[5] = jnp.exp(last) * ones
    copies[0].wait()
    z = jnp.dot(normed[...], zgate_v[...], preferred_element_type=f32)
    silu[...] = z * jax.nn.sigmoid(z)
    copies[1].wait()
    value[...] = jnp.dot(normed[...], value_v[...], preferred_element_type=f32)


def solve_kernel(
    own, one, three, two, value, silu, aux, gain, out_w, part, squares, update_out,
    key_scale_out, sent,
):
    total, grams = own[: 2 * TOKS], own[2 * TOKS :]
    for piece in (one, three, two):
        total = total + piece[: 2 * TOKS].astype(f32)
        grams = grams + decoded(piece[2 * TOKS :])
    key_gram, cross_gram = grams[:, :LANES], grams[:, LANES:]
    t = lax.broadcasted_iota(jnp.int32, (TOKS, LANES), 0)
    j = lax.broadcasted_iota(jnp.int32, (TOKS, LANES), 1)
    diagonal = jnp.where(t == j, key_gram, 0.0)
    key_col = lax.rsqrt(jnp.sum(diagonal, axis=1, keepdims=True) + epsilon)
    key_row = lax.rsqrt(jnp.sum(diagonal, axis=0, keepdims=True) + epsilon)
    length = jnp.sum(jnp.where(j == TOKS, key_gram, 0.0), axis=1, keepdims=True)
    query_col = lax.rsqrt(length + epsilon) * DK ** (-0.5)
    key_scale_out[...] = key_col * jnp.ones((TOKS, LANES), f32)
    lower = aux[0] * key_gram * key_col * key_row
    mixing = aux[1] * cross_gram * query_col * key_row
    strength, grown, leftover = aux[2][:, :1], aux[3][:, :1], aux[4][:, :1]
    rest = strength * (value[...] - grown * (total[:TOKS] * key_col))
    readout = grown * (total[TOKS:] * query_col)
    solved = []
    for k in range(TOKS):
        update = rest[k : k + 1]
        solved.append(update)
        if k < TOKS - 1:
            rest = rest - lower[:, k : k + 1] * update
        readout = readout + mixing[:, k : k + 1] * update
    gated = (readout * gain[...] * silu[...]).astype(bf16)
    partial = jnp.dot(gated, out_w[...], preferred_element_type=f32)
    width, columns = partial.shape[1], readout.shape[1]
    part[...] = partial
    sent[:, :width] = partial.astype(bf16)
    solved = leftover * jnp.concatenate(solved, axis=0)
    update_out[...] = solved
    sent[:, width : width + columns] = solved.astype(bf16)
    square = jnp.sum(readout * readout, axis=-1, keepdims=True) * jnp.ones((TOKS, LANES), f32)
    squares[...] = square
    sent[:, width + columns :] = coded(square)


def state_kernel(state, key, key_scale, updates, one, three, two, aux, out, wide):
    place = lax.axis_index(X)
    columns = updates.shape[1]
    start = one.shape[1] - LANES - columns
    wide[:, block_of(place, columns)] = updates[...]
    for step, piece in zip(STEPS, (one, three, two)):
        wide[:, block_of(place ^ step, columns)] = piece[:, start : start + columns].astype(f32)
    normalized = key[...] * key_scale[:, :1]
    added = lax.dot_general(
        normalized, wide[...], (((0,), (0,)), ((), ())), precision=HIGHEST,
        preferred_element_type=f32,
    )
    out[...] = aux[5][:1, :1] * state[...] + added


def rows_sum_kernel(part, squares, one, three, two, total, sent):
    width = part.shape[1]
    square, layer = squares[...], part[...]
    for piece in (one, three, two):
        layer = layer + piece[:, :width].astype(f32)
        square = square + decoded(piece[:, piece.shape[1] - LANES :])
    result = layer * lax.rsqrt(square[:, :1] / DK + epsilon)
    total[...] = result
    sent[...] = result.astype(bf16)


def final_kernel(total, one, three, two, hidden, gain, out):
    layer = (total[...] + two[...].astype(f32)) + (one[...].astype(f32) + three[...].astype(f32))
    stream = hidden[...].astype(f32) + layer
    inverse = lax.rsqrt(jnp.mean(stream * stream, axis=-1, keepdims=True) + epsilon)
    out[...] = (stream * inverse * gain[...]).astype(bf16)


def order_kernel(*blocks):
    *blocks, out = blocks
    place = lax.axis_index(Z)
    for step, block in zip((0,) + Z_STEPS, blocks):
        out[place ^ step] = block[...]


def near_kernel(inputs, vocab_w, logits, lse):
    result = jnp.dot(inputs[...], vocab_w[...], preferred_element_type=f32)
    logits[...] = result
    peak = jnp.max(result, axis=-1, keepdims=True)
    total = peak + jnp.log(jnp.sum(jnp.exp(result - peak), axis=-1, keepdims=True))
    lse[...] = jnp.transpose(jnp.broadcast_to(total, (LANES, LANES)))[:8]


def far_kernel(inputs, vocab_w, near_lse, logits, lse):
    result = jnp.dot(inputs[...], vocab_w[...], preferred_element_type=f32)
    logits[...] = result
    peak = jnp.max(result, axis=-1, keepdims=True)
    total = peak + jnp.log(jnp.sum(jnp.exp(result - peak), axis=-1, keepdims=True))
    lse[0:1] = near_lse[0:1]
    lse[1:2] = jnp.transpose(jnp.broadcast_to(total, (LANES, LANES)))[0:1]


def chip_kernel(mine, other, out):
    a = mine[...]
    b = jnp.concatenate([other[1:2], other[0:1]], axis=0)
    peak = jnp.maximum(a, b)
    both = peak + jnp.log(jnp.exp(a - peak) + jnp.exp(b - peak))
    out[...] = jnp.broadcast_to(both[None], out.shape)


def score_kernel(everyone, near, far, out):
    core = lax.axis_index(C)
    parts = jnp.concatenate([everyone[:, 0, :], everyone[:, 1, :]], axis=1)
    peak = jnp.max(parts, axis=0, keepdims=True)
    total = peak + jnp.log(jnp.sum(jnp.exp(parts - peak), axis=0, keepdims=True))
    for k, logits in enumerate((near, far)):
        row = total[:, k * LANES : (k + 1) * LANES]
        column = jnp.transpose(jnp.broadcast_to(row, (LANES, LANES)))[:, :1]
        half = core if k == 0 else 1 - core
        for z in range(8):
            cut = slice(z * TOKS, (z + 1) * TOKS)
            out[2 * z + half] = logits[cut] - column[cut]


def on_device(
    hidden,
    norm_gain,
    query_weight,
    key_weight,
    value_weight,
    zgate_weight,
    gate_weight,
    decay_rate,
    output_gain,
    output_weight,
    recurrent_state,
    final_gain,
    vocab_weight,
):
    hidden = hidden[0]
    width = hidden.shape[1]
    columns = query_weight.shape[2]
    state = recurrent_state[0, 0, 0]
    vocab = vocab_weight.shape[1]
    packet = shape((3 * TOKS, columns), bf16)
    own, *sent, normed, key = pl.pallas_call(
        project_kernel,
        out_shape=(
            shape((3 * TOKS, columns)),
            packet,
            packet,
            packet,
            shape((TOKS, width), bf16),
            shape((TOKS, columns)),
        ),
        in_specs=[HB] * 5,
        out_specs=(VM,) * 6,
        scratch_shapes=[
            pltpu.VMEM((TOKS, width), bf16),
            pltpu.VMEM((1, width), f32),
            pltpu.VMEM((width, columns), bf16),
            pltpu.VMEM((width, columns), bf16),
            pltpu.VMEM(state.shape, f32),
            pltpu.VMEM((2 * TOKS, DK), f32),
            pltpu.SemaphoreType.DMA((5,)),
        ],
        compiler_params=params(16),
        name="project",
    )(*in_hbm(hidden, norm_gain, key_weight[0], query_weight[0], state))
    one, three, two = [swapped(a, X, k) for a, k in zip(sent, STEPS)]
    silu, value, aux = pl.pallas_call(
        gate_kernel,
        out_shape=(shape((TOKS, columns)), shape((TOKS, columns)), shape((6, TOKS, LANES))),
        in_specs=[VM, HB, HB, VM, SM],
        out_specs=(VM, VM, VM),
        scratch_shapes=[
            pltpu.VMEM((width, columns), bf16),
            pltpu.VMEM((width, columns), bf16),
            pltpu.SemaphoreType.DMA((2,)),
        ],
        compiler_params=params(8),
        cost_estimate=cost(16 * 2048 * 1024, 2 << 20),
        name="gates",
    )(normed, *in_hbm(zgate_weight[0], value_weight[0]), gate_weight[0, :, :, 0], decay_rate)
    part, squares, updates, key_scale, sent = pl.pallas_call(
        solve_kernel,
        out_shape=(
            shape((TOKS, width)),
            shape((TOKS, LANES)),
            shape((TOKS, columns)),
            shape((TOKS, LANES)),
            shape((TOKS, width + columns + LANES), bf16),
        ),
        in_specs=[VM] * 9,
        out_specs=(VM,) * 5,
        compiler_params=params(8),
        name="solve",
    )(own, one, three, two, value, silu, aux, output_gain, output_weight[0])
    one, three, two = [swapped(sent, X, k) for k in STEPS]
    total, sent = pl.pallas_call(
        rows_sum_kernel,
        out_shape=(shape((TOKS, width)), shape((TOKS, width), bf16)),
        in_specs=[VM] * 5,
        out_specs=(VM, VM),
        compiler_params=params(4),
        name="rows_sum",
    )(part, squares, one, three, two)
    new_state = pl.pallas_call(
        state_kernel,
        out_shape=shape(state.shape),
        in_specs=[VM] * 8,
        out_specs=VM,
        scratch_shapes=[pltpu.VMEM((TOKS, DK), f32)],
        compiler_params=params(8),
        cost_estimate=cost(2 * 16 * 256 * 1024 * 6, 2 << 20),
        name="next_state",
    )(state, key, key_scale, updates, one, three, two, aux)
    one, three, two = [swapped(sent, Y, k) for k in STEPS]
    one, three, two, new_state = lax.optimization_barrier((one, three, two, new_state))
    final_in = pl.pallas_call(
        final_kernel,
        out_shape=shape((TOKS, width), bf16),
        in_specs=[VM] * 6,
        out_specs=VM,
        compiler_params=params(4),
        name="final_norm",
    )(total, one, three, two, hidden, final_gain[None])
    near = pl.pallas_call(
        order_kernel,
        out_shape=shape((8, TOKS, width), bf16),
        in_specs=[VM] * 8,
        out_specs=VM,
        compiler_params=params(4),
        name="ordered",
    )(final_in, *(swapped(final_in, Z, k) for k in Z_STEPS)).reshape(LANES, width)
    far = swapped(near, C, 1)
    near_logits, near_lse = pl.pallas_call(
        near_kernel,
        out_shape=(shape((LANES, vocab)), shape((8, LANES))),
        in_specs=[VM, VM],
        out_specs=(VM, VM),
        compiler_params=params(16),
        cost_estimate=cost(2 * 128 * 2048 * 512, 3 << 20),
        name="near_scores",
    )(near, vocab_weight)
    far_logits, lse = pl.pallas_call(
        far_kernel,
        out_shape=(shape((LANES, vocab)), shape((2, LANES))),
        in_specs=[VM, VM, VM],
        out_specs=(VM, VM),
        compiler_params=params(16),
        cost_estimate=cost(2 * 128 * 2048 * 512, 3 << 20),
        name="far_scores",
    )(far, vocab_weight, near_lse)
    other = swapped(lse, C, 1)
    chip = pl.pallas_call(
        chip_kernel,
        out_shape=shape((LANES, 2, LANES)),
        in_specs=[VM, VM],
        out_specs=VM,
        compiler_params=params(4),
        name="chip_total",
    )(lse, other)
    everyone = exchanged(chip, (Z, X, Y))
    log_probs = pl.pallas_call(
        score_kernel,
        out_shape=shape((16, TOKS, vocab)),
        in_specs=[VM] * 3,
        out_specs=VM,
        compiler_params=params(8),
        name="log_probs",
    )(everyone, near_logits, far_logits)
    return (new_state[None, None, None], log_probs)


def solution(mesh):
    split = Mesh(
        mesh.devices.reshape(8, 2, mesh.shape["rows"], mesh.shape["heads"]),
        ALL,
    )
    return jax.shard_map(
        on_device,
        mesh=split,
        in_specs=(
            P(DP, None, None),
            P(),
            P(None, None, (Y, X)),
            P(None, None, (Y, X)),
            P(None, None, (Y, X)),
            P(None, None, (Y, X)),
            P(None, None, None, Y),
            P(None, Y),
            P(None, X),
            P(None, (Y, X), None),
            P(None, DP, Y, X, None),
            P(),
            P(None, ALL),
        ),
        out_specs=(P(None, DP, Y, X, None), P(None, None, ALL)),
        check_vma=False,
    )
```

```python
import jax
import jax.numpy as jnp
from jax import lax
from jax.experimental import pallas as pl
from jax.experimental.pallas import tpu as pltpu
from jax.sharding import Mesh
from jax.sharding import PartitionSpec as P

Z, C, X, Y = ("dp_0", "dp_1", "rows", "heads")
DP = (Z, C)
ALL = (Z, C, X, Y)

TOKS = 16
DK = 1024
LANES = 128
epsilon = 1e-06
STEPS = (2, 3, 1)
f32, bf16 = jnp.float32, jnp.bfloat16
HIGHEST = lax.Precision.HIGHEST

VM = pl.BlockSpec(memory_space=pltpu.VMEM)
SM = pl.BlockSpec(memory_space=pltpu.SMEM)
HB = pl.BlockSpec(memory_space=pltpu.HBM)


def exchanged(parts, axes):
    return lax.all_to_all(parts, axes, 0, 0, tiled=True)


def swapped(shard, axis, step):
    return lax.ppermute(shard, axis, [(i, i ^ step) for i in range(lax.axis_size(axis))])


def in_hbm(*arrays):
    return [pltpu.with_memory_space_constraint(a, pltpu.HBM) for a in arrays]


def shape(dims, dtype=f32):
    return jax.ShapeDtypeStruct(dims, dtype)


def params(mib):
    return pltpu.CompilerParams(vmem_limit_bytes=mib << 20)


def cost(flops, size):
    return pl.CostEstimate(flops=flops, bytes_accessed=size, transcendentals=0)


def across(a, b):
    return lax.dot_general(
        a, b, (((1,), (1,)), ((), ())), precision=HIGHEST, preferred_element_type=f32
    )


def halves(a):
    high = a.astype(bf16)
    return high, (a - high.astype(f32)).astype(bf16)


def coded(a):
    high, low = halves(a)
    lane = lax.broadcasted_iota(jnp.int32, a.shape, 1) % LANES
    return jnp.where(lane < 64, high.astype(f32), pltpu.roll(low.astype(f32), 64, 1)).astype(bf16)


def decoded(a):
    a = a.astype(f32)
    return a + pltpu.roll(a, a.shape[1] - 64, 1)


def block_of(device, size):
    return pl.ds(pl.multiple_of(device * size, size), size)


def project_kernel(
    hidden, gain, key_w, query_w, state, own, sent_a, sent_b, sent_c, normed, key_out,
    hidden_v, gain_v, key_v, query_v, state_v, wide, sems,
):
    pairs = (
        (hidden, hidden_v), (gain, gain_v), (key_w, key_v), (query_w, query_v),
        (state, state_v),
    )
    copies = [pltpu.make_async_copy(a, b, sems.at[i]) for i, (a, b) in enumerate(pairs)]
    for copy in copies:
        copy.start()
    copies[0].wait()
    copies[1].wait()
    x = hidden_v[...].astype(f32)
    inverse = lax.rsqrt(jnp.mean(x * x, axis=-1, keepdims=True) + epsilon)
    inputs = (x * inverse * gain_v[...]).astype(bf16)
    normed[...] = inputs
    copies[2].wait()
    key = jnp.dot(inputs, key_v[...], preferred_element_type=f32)
    key_out[...] = key
    copies[3].wait()
    query = jnp.dot(inputs, query_v[...], preferred_element_type=f32)
    both = jnp.concatenate([key, query], axis=0)
    wide_key = jnp.concatenate([key, jnp.zeros((LANES - TOKS, key.shape[1]), f32)], axis=0)
    grams = across(both, wide_key)
    length = jnp.sum(query * query, axis=-1, keepdims=True)
    lane = lax.broadcasted_iota(jnp.int32, (TOKS, LANES), 1)
    grams = jnp.concatenate(
        [jnp.where(lane == TOKS, length, grams[:TOKS]), grams[TOKS:]], axis=1
    )
    own[2 * TOKS :] = grams
    grams = coded(grams)
    high, low = halves(both)
    copies[4].wait()
    state_high, state_low = halves(state_v[...])
    first = jnp.dot(jnp.concatenate([high, low], axis=0), state_high, preferred_element_type=f32)
    second = jnp.dot(high, state_low, preferred_element_type=f32)
    wide[...] = first[: 2 * TOKS] + first[2 * TOKS :] + second
    place, columns = lax.axis_index(X), key.shape[1]
    own[: 2 * TOKS] = wide[:, block_of(place, columns)]
    for step, sent in zip(STEPS, (sent_a, sent_b, sent_c)):
        sent[: 2 * TOKS] = wide[:, block_of(place ^ step, columns)].astype(bf16)
        sent[2 * TOKS :] = grams


def gate_kernel(
    normed, zgate_w, value_w, gate_w, rate, silu, value, aux, zgate_v, value_v, sems,
):
    copies = [
        pltpu.make_async_copy(zgate_w, zgate_v, sems.at[0]),
        pltpu.make_async_copy(value_w, value_v, sems.at[1]),
    ]
    for copy in copies:
        copy.start()
    inputs = normed[...]
    inputs = inputs.astype(f32)
    gates = gate_w[...].astype(f32)
    decay_in = jnp.sum(inputs * gates[0:1], axis=-1, keepdims=True)
    strength = jax.nn.sigmoid(jnp.sum(inputs * gates[1:2], axis=-1, keepdims=True))
    softplus = jnp.maximum(decay_in, 0.0) + jnp.log1p(jnp.exp(-jnp.abs(decay_in)))
    decay = -rate[0, 0] * softplus
    t = lax.broadcasted_iota(jnp.int32, (TOKS, LANES), 0)
    j = lax.broadcasted_iota(jnp.int32, (TOKS, LANES), 1)
    decay_row = jnp.sum(jnp.where(t == j, decay, 0.0), axis=0, keepdims=True)
    log_col = jnp.sum(jnp.where(j <= t, decay_row, 0.0), axis=1, keepdims=True)
    log_row = jnp.sum(jnp.where(t <= j, decay, 0.0), axis=0, keepdims=True)
    causal = j <= t
    ratio = jnp.where(causal, jnp.exp(jnp.where(causal, log_col - log_row, 0.0)), 0.0)
    last = jnp.sum(decay, axis=0, keepdims=True)
    ones = jnp.ones((TOKS, LANES), f32)
    aux[0] = jnp.where(j < t, strength * ratio, 0.0)
    aux[1] = ratio
    aux[2] = strength * ones
    aux[3] = jnp.exp(log_col) * ones
    aux[4] = jnp.exp(last - log_col) * ones
    aux[5] = jnp.exp(last) * ones
    copies[0].wait()
    z = jnp.dot(normed[...], zgate_v[...], preferred_element_type=f32)
    silu[...] = z * jax.nn.sigmoid(z)
    copies[1].wait()
    value[...] = jnp.dot(normed[...], value_v[...], preferred_element_type=f32)


def solve_kernel(
    own, part_a, part_b, part_c, value, silu, aux, gain, out_w, part, squares, update_out,
    key_scale_out, sent,
):
    total, grams = own[: 2 * TOKS], own[2 * TOKS :]
    for piece in (part_a, part_b, part_c):
        total = total + piece[: 2 * TOKS].astype(f32)
        grams = grams + decoded(piece[2 * TOKS :])
    key_gram, cross_gram = grams[:, :LANES], grams[:, LANES:]
    t = lax.broadcasted_iota(jnp.int32, (TOKS, LANES), 0)
    j = lax.broadcasted_iota(jnp.int32, (TOKS, LANES), 1)
    diagonal = jnp.where(t == j, key_gram, 0.0)
    key_col = lax.rsqrt(jnp.sum(diagonal, axis=1, keepdims=True) + epsilon)
    key_row = lax.rsqrt(jnp.sum(diagonal, axis=0, keepdims=True) + epsilon)
    length = jnp.sum(jnp.where(j == TOKS, key_gram, 0.0), axis=1, keepdims=True)
    query_col = lax.rsqrt(length + epsilon) * DK ** (-0.5)
    key_scale_out[...] = key_col * jnp.ones((TOKS, LANES), f32)
    lower = aux[0] * key_gram * key_col * key_row
    mixing = aux[1] * cross_gram * query_col * key_row
    strength, grown, leftover = aux[2][:, :1], aux[3][:, :1], aux[4][:, :1]
    rest = strength * (value[...] - grown * (total[:TOKS] * key_col))
    readout = grown * (total[TOKS:] * query_col)
    solved = []
    for k in range(TOKS):
        update = rest[k : k + 1]
        solved.append(update)
        if k < TOKS - 1:
            rest = rest - lower[:, k : k + 1] * update
        readout = readout + mixing[:, k : k + 1] * update
    gated = (readout * gain[...] * silu[...]).astype(bf16)
    partial = jnp.dot(gated, out_w[...], preferred_element_type=f32)
    width, columns = partial.shape[1], readout.shape[1]
    part[...] = partial
    sent[:, :width] = partial.astype(bf16)
    solved = leftover * jnp.concatenate(solved, axis=0)
    update_out[...] = solved
    sent[:, width : width + columns] = solved.astype(bf16)
    square = jnp.sum(readout * readout, axis=-1, keepdims=True) * jnp.ones((TOKS, LANES), f32)
    squares[...] = square
    sent[:, width + columns :] = coded(square)


def state_kernel(state, key, key_scale, updates, part_a, part_b, part_c, aux, out, wide):
    place = lax.axis_index(X)
    columns = updates.shape[1]
    start = part_a.shape[1] - LANES - columns
    wide[:, block_of(place, columns)] = updates[...]
    for step, piece in zip(STEPS, (part_a, part_b, part_c)):
        wide[:, block_of(place ^ step, columns)] = piece[:, start : start + columns].astype(f32)
    normalized = key[...] * key_scale[:, :1]
    added = lax.dot_general(
        normalized, wide[...], (((0,), (0,)), ((), ())), precision=HIGHEST,
        preferred_element_type=f32,
    )
    out[...] = aux[5][:1, :1] * state[...] + added


def rows_sum_kernel(part, squares, part_a, part_b, part_c, total, sent):
    width = part.shape[1]
    square, layer = squares[...], part[...]
    for piece in (part_a, part_b, part_c):
        layer = layer + piece[:, :width].astype(f32)
        square = square + decoded(piece[:, piece.shape[1] - LANES :])
    result = layer * lax.rsqrt(square[:, :1] / DK + epsilon)
    total[...] = result
    sent[...] = result.astype(bf16)


def final_kernel(total, part_a, part_b, part_c, hidden, gain, out):
    layer = (total[...] + part_c[...].astype(f32)) + (part_a[...].astype(f32) + part_b[...].astype(f32))
    stream = hidden[...].astype(f32) + layer
    inverse = lax.rsqrt(jnp.mean(stream * stream, axis=-1, keepdims=True) + epsilon)
    final = (stream * inverse * gain[...]).astype(bf16)
    for k in range(out.shape[0]):
        out[k] = final


def near_kernel(inputs, vocab_w, logits, lse):
    result = jnp.dot(inputs[...], vocab_w[...], preferred_element_type=f32)
    logits[...] = result
    peak = jnp.max(result, axis=-1, keepdims=True)
    total = peak + jnp.log(jnp.sum(jnp.exp(result - peak), axis=-1, keepdims=True))
    lse[...] = jnp.transpose(jnp.broadcast_to(total, (LANES, LANES)))[:8]


def far_kernel(inputs, vocab_w, near_lse, logits, lse):
    result = jnp.dot(inputs[...], vocab_w[...], preferred_element_type=f32)
    logits[...] = result
    peak = jnp.max(result, axis=-1, keepdims=True)
    total = peak + jnp.log(jnp.sum(jnp.exp(result - peak), axis=-1, keepdims=True))
    lse[0:1] = near_lse[0:1]
    lse[1:2] = jnp.transpose(jnp.broadcast_to(total, (LANES, LANES)))[0:1]


def chip_kernel(mine, other, out):
    a = mine[...]
    b = jnp.concatenate([other[1:2], other[0:1]], axis=0)
    peak = jnp.maximum(a, b)
    both = peak + jnp.log(jnp.exp(a - peak) + jnp.exp(b - peak))
    out[...] = jnp.broadcast_to(both[None], out.shape)


def score_kernel(everyone, near, far, out):
    core = lax.axis_index(C)
    parts = jnp.concatenate([everyone[:, 0, :], everyone[:, 1, :]], axis=1)
    peak = jnp.max(parts, axis=0, keepdims=True)
    total = peak + jnp.log(jnp.sum(jnp.exp(parts - peak), axis=0, keepdims=True))
    for k, logits in enumerate((near, far)):
        row = total[:, k * LANES : (k + 1) * LANES]
        column = jnp.transpose(jnp.broadcast_to(row, (LANES, LANES)))[:, :1]
        half = core if k == 0 else 1 - core
        for z in range(8):
            cut = slice(z * TOKS, (z + 1) * TOKS)
            out[2 * z + half] = logits[cut] - column[cut]


def on_device(
    hidden,
    norm_gain,
    query_weight,
    key_weight,
    value_weight,
    zgate_weight,
    gate_weight,
    decay_rate,
    output_gain,
    output_weight,
    recurrent_state,
    final_gain,
    vocab_weight,
):
    hidden = hidden[0]
    width = hidden.shape[1]
    columns = query_weight.shape[2]
    state = recurrent_state[0, 0, 0]
    vocab = vocab_weight.shape[1]
    packet = shape((3 * TOKS, columns), bf16)
    own, *sent, normed, key = pl.pallas_call(
        project_kernel,
        out_shape=(
            shape((3 * TOKS, columns)),
            packet,
            packet,
            packet,
            shape((TOKS, width), bf16),
            shape((TOKS, columns)),
        ),
        in_specs=[HB] * 5,
        out_specs=(VM,) * 6,
        scratch_shapes=[
            pltpu.VMEM((TOKS, width), bf16),
            pltpu.VMEM((1, width), f32),
            pltpu.VMEM((width, columns), bf16),
            pltpu.VMEM((width, columns), bf16),
            pltpu.VMEM(state.shape, f32),
            pltpu.VMEM((2 * TOKS, DK), f32),
            pltpu.SemaphoreType.DMA((5,)),
        ],
        compiler_params=params(16),
        name="project",
    )(*in_hbm(hidden, norm_gain, key_weight[0], query_weight[0], state))
    part_a, part_b, part_c = [swapped(a, X, k) for a, k in zip(sent, STEPS)]
    silu, value, aux = pl.pallas_call(
        gate_kernel,
        out_shape=(shape((TOKS, columns)), shape((TOKS, columns)), shape((6, TOKS, LANES))),
        in_specs=[VM, HB, HB, VM, SM],
        out_specs=(VM, VM, VM),
        scratch_shapes=[
            pltpu.VMEM((width, columns), bf16),
            pltpu.VMEM((width, columns), bf16),
            pltpu.SemaphoreType.DMA((2,)),
        ],
        compiler_params=params(8),
        cost_estimate=cost(16 * 2048 * 1024, 2 << 20),
        name="gates",
    )(normed, *in_hbm(zgate_weight[0], value_weight[0]), gate_weight[0, :, :, 0], decay_rate)
    part, squares, updates, key_scale, sent = pl.pallas_call(
        solve_kernel,
        out_shape=(
            shape((TOKS, width)),
            shape((TOKS, LANES)),
            shape((TOKS, columns)),
            shape((TOKS, LANES)),
            shape((TOKS, width + columns + LANES), bf16),
        ),
        in_specs=[VM] * 9,
        out_specs=(VM,) * 5,
        compiler_params=params(8),
        name="solve",
    )(own, part_a, part_b, part_c, value, silu, aux, output_gain, output_weight[0])
    part_a, part_b, part_c = [swapped(sent, X, k) for k in STEPS]
    total, sent = pl.pallas_call(
        rows_sum_kernel,
        out_shape=(shape((TOKS, width)), shape((TOKS, width), bf16)),
        in_specs=[VM] * 5,
        out_specs=(VM, VM),
        compiler_params=params(4),
        name="rows_sum",
    )(part, squares, part_a, part_b, part_c)
    new_state = pl.pallas_call(
        state_kernel,
        out_shape=shape(state.shape),
        in_specs=[VM] * 8,
        out_specs=VM,
        scratch_shapes=[pltpu.VMEM((TOKS, DK), f32)],
        compiler_params=params(8),
        cost_estimate=cost(2 * 16 * 256 * 1024 * 6, 2 << 20),
        name="next_state",
    )(state, key, key_scale, updates, part_a, part_b, part_c, aux)
    part_a, part_b, part_c = [swapped(sent, Y, k) for k in STEPS]
    part_a, part_b, part_c, new_state = lax.optimization_barrier((part_a, part_b, part_c, new_state))
    final_in = pl.pallas_call(
        final_kernel,
        out_shape=shape((8, TOKS, width), bf16),
        in_specs=[VM] * 6,
        out_specs=VM,
        compiler_params=params(4),
        name="final_norm",
    )(total, part_a, part_b, part_c, hidden, final_gain[None])
    near = exchanged(final_in, Z).reshape(LANES, width)
    far = swapped(near, C, 1)
    near_logits, near_lse = pl.pallas_call(
        near_kernel,
        out_shape=(shape((LANES, vocab)), shape((8, LANES))),
        in_specs=[VM, VM],
        out_specs=(VM, VM),
        compiler_params=params(16),
        cost_estimate=cost(2 * 128 * 2048 * 512, 3 << 20),
        name="near_scores",
    )(near, vocab_weight)
    far_logits, lse = pl.pallas_call(
        far_kernel,
        out_shape=(shape((LANES, vocab)), shape((2, LANES))),
        in_specs=[VM, VM, VM],
        out_specs=(VM, VM),
        compiler_params=params(16),
        cost_estimate=cost(2 * 128 * 2048 * 512, 3 << 20),
        name="far_scores",
    )(far, vocab_weight, near_lse)
    other = swapped(lse, C, 1)
    chip = pl.pallas_call(
        chip_kernel,
        out_shape=shape((LANES, 2, LANES)),
        in_specs=[VM, VM],
        out_specs=VM,
        compiler_params=params(4),
        name="chip_total",
    )(lse, other)
    everyone = exchanged(chip, (Z, X, Y))
    log_probs = pl.pallas_call(
        score_kernel,
        out_shape=shape((16, TOKS, vocab)),
        in_specs=[VM] * 3,
        out_specs=VM,
        compiler_params=params(8),
        name="log_probs",
    )(everyone, near_logits, far_logits)
    return (new_state[None, None, None], log_probs)


def solution(mesh):
    split = Mesh(
        mesh.devices.reshape(8, 2, mesh.shape["rows"], mesh.shape["heads"]),
        ALL,
    )
    return jax.shard_map(
        on_device,
        mesh=split,
        in_specs=(
            P(DP, None, None),
            P(),
            P(None, None, (Y, X)),
            P(None, None, (Y, X)),
            P(None, None, (Y, X)),
            P(None, None, (Y, X)),
            P(None, None, None, Y),
            P(None, Y),
            P(None, X),
            P(None, (Y, X), None),
            P(None, DP, Y, X, None),
            P(),
            P(None, ALL),
        ),
        out_specs=(P(None, DP, Y, X, None), P(None, None, ALL)),
        check_vma=False,
    )
```

```python
import jax
import jax.numpy as jnp
from jax import lax
from jax.experimental import pallas as pl
from jax.experimental.pallas import tpu as pltpu
from jax.sharding import Mesh
from jax.sharding import PartitionSpec as P

Z, C, X, Y = ("dp_0", "dp_1", "rows", "heads")
DP = (Z, C)
ALL = (Z, C, X, Y)

TOKS = 16
DK = 1024
LANES = 128
epsilon = 1e-06
STEPS = (2, 3, 1)
f32, bf16 = jnp.float32, jnp.bfloat16
HIGHEST = lax.Precision.HIGHEST

VM = pl.BlockSpec(memory_space=pltpu.VMEM)
SM = pl.BlockSpec(memory_space=pltpu.SMEM)
HB = pl.BlockSpec(memory_space=pltpu.HBM)


def exchanged(parts, axes):
    return lax.all_to_all(parts, axes, 0, 0, tiled=True)


def swapped(shard, axis, step):
    return lax.ppermute(shard, axis, [(i, i ^ step) for i in range(lax.axis_size(axis))])


def in_hbm(*arrays):
    return [pltpu.with_memory_space_constraint(a, pltpu.HBM) for a in arrays]


def shape(dims, dtype=f32):
    return jax.ShapeDtypeStruct(dims, dtype)


def params(mib):
    return pltpu.CompilerParams(vmem_limit_bytes=mib << 20)


def cost(flops, size):
    return pl.CostEstimate(flops=flops, bytes_accessed=size, transcendentals=0)


def across(a, b):
    return lax.dot_general(
        a, b, (((1,), (1,)), ((), ())), precision=HIGHEST, preferred_element_type=f32
    )


def halves(a):
    high = a.astype(bf16)
    return high, (a - high.astype(f32)).astype(bf16)


def coded(a):
    high, low = halves(a)
    lane = lax.broadcasted_iota(jnp.int32, a.shape, 1) % LANES
    return jnp.where(lane < 64, high.astype(f32), pltpu.roll(low.astype(f32), 64, 1)).astype(bf16)


def decoded(a):
    a = a.astype(f32)
    return a + pltpu.roll(a, a.shape[1] - 64, 1)


def block_of(device, size):
    return pl.ds(pl.multiple_of(device * size, size), size)


def project_kernel(
    hidden, gain, key_w, query_w, state, own, sent_a, sent_b, sent_c, normed, key_out,
    hidden_v, gain_v, key_v, query_v, state_v, wide, sems,
):
    pairs = (
        (hidden, hidden_v), (gain, gain_v), (key_w, key_v), (query_w, query_v),
        (state, state_v),
    )
    copies = [pltpu.make_async_copy(a, b, sems.at[i]) for i, (a, b) in enumerate(pairs)]
    for copy in copies:
        copy.start()
    copies[0].wait()
    copies[1].wait()
    x = hidden_v[...].astype(f32)
    inverse = lax.rsqrt(jnp.mean(x * x, axis=-1, keepdims=True) + epsilon)
    inputs = (x * inverse * gain_v[...]).astype(bf16)
    normed[...] = inputs
    copies[2].wait()
    key = jnp.dot(inputs, key_v[...], preferred_element_type=f32)
    key_out[...] = key
    copies[3].wait()
    query = jnp.dot(inputs, query_v[...], preferred_element_type=f32)
    both = jnp.concatenate([key, query], axis=0)
    wide_key = jnp.concatenate([key, jnp.zeros((LANES - TOKS, key.shape[1]), f32)], axis=0)
    grams = across(both, wide_key)
    length = jnp.sum(query * query, axis=-1, keepdims=True)
    lane = lax.broadcasted_iota(jnp.int32, (TOKS, LANES), 1)
    grams = jnp.concatenate(
        [jnp.where(lane == TOKS, length, grams[:TOKS]), grams[TOKS:]], axis=1
    )
    own[2 * TOKS :] = grams
    grams = coded(grams)
    high, low = halves(both)
    copies[4].wait()
    state_high, state_low = halves(state_v[...])
    first = jnp.dot(jnp.concatenate([high, low], axis=0), state_high, preferred_element_type=f32)
    second = jnp.dot(high, state_low, preferred_element_type=f32)
    wide[...] = first[: 2 * TOKS] + first[2 * TOKS :] + second
    place, columns = lax.axis_index(X), key.shape[1]
    own[: 2 * TOKS] = wide[:, block_of(place, columns)]
    for step, sent in zip(STEPS, (sent_a, sent_b, sent_c)):
        sent[: 2 * TOKS] = wide[:, block_of(place ^ step, columns)].astype(bf16)
        sent[2 * TOKS :] = grams


def gate_kernel(
    normed, zgate_w, value_w, gate_w, rate, silu, value, aux, zgate_v, value_v, sems,
):
    copies = [
        pltpu.make_async_copy(zgate_w, zgate_v, sems.at[0]),
        pltpu.make_async_copy(value_w, value_v, sems.at[1]),
    ]
    for copy in copies:
        copy.start()
    inputs = normed[...]
    inputs = inputs.astype(f32)
    gates = gate_w[...].astype(f32)
    decay_in = jnp.sum(inputs * gates[0:1], axis=-1, keepdims=True)
    strength = jax.nn.sigmoid(jnp.sum(inputs * gates[1:2], axis=-1, keepdims=True))
    softplus = jnp.maximum(decay_in, 0.0) + jnp.log1p(jnp.exp(-jnp.abs(decay_in)))
    decay = -rate[0, 0] * softplus
    t = lax.broadcasted_iota(jnp.int32, (TOKS, LANES), 0)
    j = lax.broadcasted_iota(jnp.int32, (TOKS, LANES), 1)
    decay_row = jnp.sum(jnp.where(t == j, decay, 0.0), axis=0, keepdims=True)
    log_col = jnp.sum(jnp.where(j <= t, decay_row, 0.0), axis=1, keepdims=True)
    log_row = jnp.sum(jnp.where(t <= j, decay, 0.0), axis=0, keepdims=True)
    causal = j <= t
    ratio = jnp.where(causal, jnp.exp(jnp.where(causal, log_col - log_row, 0.0)), 0.0)
    last = jnp.sum(decay, axis=0, keepdims=True)
    ones = jnp.ones((TOKS, LANES), f32)
    aux[0] = jnp.where(j < t, strength * ratio, 0.0)
    aux[1] = ratio
    aux[2] = strength * ones
    aux[3] = jnp.exp(log_col) * ones
    aux[4] = jnp.exp(last - log_col) * ones
    aux[5] = jnp.exp(last) * ones
    copies[0].wait()
    z = jnp.dot(normed[...], zgate_v[...], preferred_element_type=f32)
    silu[...] = z * jax.nn.sigmoid(z)
    copies[1].wait()
    value[...] = jnp.dot(normed[...], value_v[...], preferred_element_type=f32)


def solve_kernel(
    own, part_a, part_b, part_c, value, silu, aux, gain, out_w, part, squares, update_out,
    key_scale_out, sent,
):
    total, grams = own[: 2 * TOKS], own[2 * TOKS :]
    for piece in (part_a, part_b, part_c):
        total = total + piece[: 2 * TOKS].astype(f32)
        grams = grams + decoded(piece[2 * TOKS :])
    key_gram, cross_gram = grams[:, :LANES], grams[:, LANES:]
    t = lax.broadcasted_iota(jnp.int32, (TOKS, LANES), 0)
    j = lax.broadcasted_iota(jnp.int32, (TOKS, LANES), 1)
    diagonal = jnp.where(t == j, key_gram, 0.0)
    key_col = lax.rsqrt(jnp.sum(diagonal, axis=1, keepdims=True) + epsilon)
    key_row = lax.rsqrt(jnp.sum(diagonal, axis=0, keepdims=True) + epsilon)
    length = jnp.sum(jnp.where(j == TOKS, key_gram, 0.0), axis=1, keepdims=True)
    query_col = lax.rsqrt(length + epsilon) * DK ** (-0.5)
    key_scale_out[...] = key_col * jnp.ones((TOKS, LANES), f32)
    lower = aux[0] * key_gram * key_col * key_row
    mixing = aux[1] * cross_gram * query_col * key_row
    strength, grown, leftover = aux[2][:, :1], aux[3][:, :1], aux[4][:, :1]
    rest = strength * (value[...] - grown * (total[:TOKS] * key_col))
    readout = grown * (total[TOKS:] * query_col)
    solved = []
    for k in range(TOKS):
        update = rest[k : k + 1]
        solved.append(update)
        if k < TOKS - 1:
            rest = rest - lower[:, k : k + 1] * update
        readout = readout + mixing[:, k : k + 1] * update
    gated = (readout * gain[...] * silu[...]).astype(bf16)
    partial = jnp.dot(gated, out_w[...], preferred_element_type=f32)
    width, columns = partial.shape[1], readout.shape[1]
    part[...] = partial
    sent[:, :width] = partial.astype(bf16)
    solved = leftover * jnp.concatenate(solved, axis=0)
    update_out[...] = solved
    sent[:, width : width + columns] = solved.astype(bf16)
    square = jnp.sum(readout * readout, axis=-1, keepdims=True) * jnp.ones((TOKS, LANES), f32)
    squares[...] = square
    sent[:, width + columns :] = coded(square)


def state_kernel(state, key, key_scale, updates, part_a, part_b, part_c, aux, out, wide):
    place = lax.axis_index(X)
    columns = updates.shape[1]
    start = part_a.shape[1] - LANES - columns
    wide[:, block_of(place, columns)] = updates[...]
    for step, piece in zip(STEPS, (part_a, part_b, part_c)):
        wide[:, block_of(place ^ step, columns)] = piece[:, start : start + columns].astype(f32)
    normalized = key[...] * key_scale[:, :1]
    added = lax.dot_general(
        normalized, wide[...], (((0,), (0,)), ((), ())), precision=HIGHEST,
        preferred_element_type=f32,
    )
    out[...] = aux[5][:1, :1] * state[...] + added


def rows_sum_kernel(part, squares, part_a, part_b, part_c, total, sent):
    width = part.shape[1]
    square, layer = squares[...], part[...]
    for piece in (part_a, part_b, part_c):
        layer = layer + piece[:, :width].astype(f32)
        square = square + decoded(piece[:, piece.shape[1] - LANES :])
    result = layer * lax.rsqrt(square[:, :1] / DK + epsilon)
    total[...] = result
    sent[...] = result.astype(bf16)


def final_kernel(total, part_a, part_b, part_c, hidden, gain, low, high):
    layer = (total[...] + part_c[...].astype(f32)) + (part_a[...].astype(f32) + part_b[...].astype(f32))
    stream = hidden[...].astype(f32) + layer
    inverse = lax.rsqrt(jnp.mean(stream * stream, axis=-1, keepdims=True) + epsilon)
    final = stream * inverse * gain[...]
    rows = low.shape[1]
    for k in range(low.shape[0]):
        low[k] = final[:rows].astype(bf16)
        high[k] = final[rows:].astype(bf16)


def scores_kernel(inputs, vocab_w, logits, lse):
    result = jnp.dot(inputs[...], vocab_w[...], preferred_element_type=f32)
    logits[...] = result
    lse[...] = log_sum_exp(result)


def last_scores_kernel(inputs, vocab_w, near_low, near_high, far_low, logits, lse):
    result = jnp.dot(inputs[...], vocab_w[...], preferred_element_type=f32)
    logits[...] = result
    near = jnp.concatenate([near_low[...], near_high[...]], axis=0)
    far = jnp.concatenate([far_low[...], log_sum_exp(result)], axis=0)
    lse[0:1] = jnp.transpose(near)[0:1]
    lse[1:2] = jnp.transpose(far)[0:1]


def log_sum_exp(logits):
    peak = jnp.max(logits, axis=-1, keepdims=True)
    total = peak + jnp.log(jnp.sum(jnp.exp(logits - peak), axis=-1, keepdims=True))
    return jnp.broadcast_to(total, (logits.shape[0], LANES))


def chip_kernel(mine, other, out):
    a = mine[...]
    b = jnp.concatenate([other[1:2], other[0:1]], axis=0)
    peak = jnp.maximum(a, b)
    both = peak + jnp.log(jnp.exp(a - peak) + jnp.exp(b - peak))
    out[...] = jnp.broadcast_to(both[None], out.shape)


def score_kernel(everyone, near_low, near_high, far_low, far_high, out):
    core = lax.axis_index(C)
    parts = jnp.concatenate([everyone[:, 0, :], everyone[:, 1, :]], axis=1)
    peak = jnp.max(parts, axis=0, keepdims=True)
    total = peak + jnp.log(jnp.sum(jnp.exp(parts - peak), axis=0, keepdims=True))
    for k, halves_of in enumerate(((near_low, near_high), (far_low, far_high))):
        row = total[:, k * LANES : (k + 1) * LANES]
        column = jnp.transpose(jnp.broadcast_to(row, (LANES, LANES)))[:, :1]
        half = core if k == 0 else 1 - core
        for m, logits in enumerate(halves_of):
            count = logits.shape[0]
            size = count // 8
            for z in range(8):
                cut = slice(z * size, (z + 1) * size)
                shift = column[m * count + z * size : m * count + (z + 1) * size]
                out[2 * z + half, m * size : (m + 1) * size] = logits[cut] - shift


def on_device(
    hidden,
    norm_gain,
    query_weight,
    key_weight,
    value_weight,
    zgate_weight,
    gate_weight,
    decay_rate,
    output_gain,
    output_weight,
    recurrent_state,
    final_gain,
    vocab_weight,
):
    hidden = hidden[0]
    width = hidden.shape[1]
    columns = query_weight.shape[2]
    state = recurrent_state[0, 0, 0]
    vocab = vocab_weight.shape[1]
    packet = shape((3 * TOKS, columns), bf16)
    own, *sent, normed, key = pl.pallas_call(
        project_kernel,
        out_shape=(
            shape((3 * TOKS, columns)),
            packet,
            packet,
            packet,
            shape((TOKS, width), bf16),
            shape((TOKS, columns)),
        ),
        in_specs=[HB] * 5,
        out_specs=(VM,) * 6,
        scratch_shapes=[
            pltpu.VMEM((TOKS, width), bf16),
            pltpu.VMEM((1, width), f32),
            pltpu.VMEM((width, columns), bf16),
            pltpu.VMEM((width, columns), bf16),
            pltpu.VMEM(state.shape, f32),
            pltpu.VMEM((2 * TOKS, DK), f32),
            pltpu.SemaphoreType.DMA((5,)),
        ],
        compiler_params=params(16),
        name="project",
    )(*in_hbm(hidden, norm_gain, key_weight[0], query_weight[0], state))
    part_a, part_b, part_c = [swapped(a, X, k) for a, k in zip(sent, STEPS)]
    silu, value, aux = pl.pallas_call(
        gate_kernel,
        out_shape=(shape((TOKS, columns)), shape((TOKS, columns)), shape((6, TOKS, LANES))),
        in_specs=[VM, HB, HB, VM, SM],
        out_specs=(VM, VM, VM),
        scratch_shapes=[
            pltpu.VMEM((width, columns), bf16),
            pltpu.VMEM((width, columns), bf16),
            pltpu.SemaphoreType.DMA((2,)),
        ],
        compiler_params=params(8),
        cost_estimate=cost(16 * 2048 * 1024, 2 << 20),
        name="gates",
    )(normed, *in_hbm(zgate_weight[0], value_weight[0]), gate_weight[0, :, :, 0], decay_rate)
    part, squares, updates, key_scale, sent = pl.pallas_call(
        solve_kernel,
        out_shape=(
            shape((TOKS, width)),
            shape((TOKS, LANES)),
            shape((TOKS, columns)),
            shape((TOKS, LANES)),
            shape((TOKS, width + columns + LANES), bf16),
        ),
        in_specs=[VM] * 9,
        out_specs=(VM,) * 5,
        compiler_params=params(8),
        name="solve",
    )(own, part_a, part_b, part_c, value, silu, aux, output_gain, output_weight[0])
    part_a, part_b, part_c = [swapped(sent, X, k) for k in STEPS]
    total, sent = pl.pallas_call(
        rows_sum_kernel,
        out_shape=(shape((TOKS, width)), shape((TOKS, width), bf16)),
        in_specs=[VM] * 5,
        out_specs=(VM, VM),
        compiler_params=params(4),
        name="rows_sum",
    )(part, squares, part_a, part_b, part_c)
    new_state = pl.pallas_call(
        state_kernel,
        out_shape=shape(state.shape),
        in_specs=[VM] * 8,
        out_specs=VM,
        scratch_shapes=[pltpu.VMEM((TOKS, DK), f32)],
        compiler_params=params(8),
        cost_estimate=cost(2 * 16 * 256 * 1024 * 6, 2 << 20),
        name="next_state",
    )(state, key, key_scale, updates, part_a, part_b, part_c, aux)
    part_a, part_b, part_c = [swapped(sent, Y, k) for k in STEPS]
    part_a, part_b, part_c, new_state = lax.optimization_barrier((part_a, part_b, part_c, new_state))
    halves_in = pl.pallas_call(
        final_kernel,
        out_shape=(shape((8, TOKS // 2, width), bf16),) * 2,
        in_specs=[VM] * 6,
        out_specs=(VM, VM),
        compiler_params=params(4),
        name="final_norm",
    )(total, part_a, part_b, part_c, hidden, final_gain[None])
    rows = LANES // 2
    near = [exchanged(half, Z).reshape(rows, width) for half in halves_in]
    far = [swapped(half, C, 1) for half in near]

    def scores(inputs, *lses):
        kernel = last_scores_kernel if lses else scores_kernel
        return pl.pallas_call(
            kernel,
            out_shape=(shape((rows, vocab)), shape((2 if lses else rows, LANES))),
            in_specs=[VM] * (2 + len(lses)),
            out_specs=(VM, VM),
            compiler_params=params(8),
            cost_estimate=cost(2 * 64 * 2048 * 512, 3 << 20),
            name="last_scores" if lses else "scores",
        )(inputs, vocab_weight, *lses)

    near_low, near_low_lse = scores(near[0])
    far_low, far_low_lse = scores(far[0])
    near_high, near_high_lse = scores(near[1])
    far_high, lse = scores(far[1], near_low_lse, near_high_lse, far_low_lse)
    other = swapped(lse, C, 1)
    chip = pl.pallas_call(
        chip_kernel,
        out_shape=shape((LANES, 2, LANES)),
        in_specs=[VM, VM],
        out_specs=VM,
        compiler_params=params(4),
        name="chip_total",
    )(lse, other)
    everyone = exchanged(chip, (Z, X, Y))
    log_probs = pl.pallas_call(
        score_kernel,
        out_shape=shape((16, TOKS, vocab)),
        in_specs=[VM] * 5,
        out_specs=VM,
        compiler_params=params(8),
        name="log_probs",
    )(everyone, near_low, near_high, far_low, far_high)
    return (new_state[None, None, None], log_probs)


def solution(mesh):
    split = Mesh(
        mesh.devices.reshape(8, 2, mesh.shape["rows"], mesh.shape["heads"]),
        ALL,
    )
    return jax.shard_map(
        on_device,
        mesh=split,
        in_specs=(
            P(DP, None, None),
            P(),
            P(None, None, (Y, X)),
            P(None, None, (Y, X)),
            P(None, None, (Y, X)),
            P(None, None, (Y, X)),
            P(None, None, None, Y),
            P(None, Y),
            P(None, X),
            P(None, (Y, X), None),
            P(None, DP, Y, X, None),
            P(),
            P(None, ALL),
        ),
        out_specs=(P(None, DP, Y, X, None), P(None, None, ALL)),
        check_vma=False,
    )
```
